32 devices in a mesh: depth: 16 (over z, y, core), filt: 2 (over x).
Axes of the slice: x: 2, y: 2, z: 4, core: 2. Of those that a mesh axis runs over, the one named last changes fastest.
Arguments:
- volume: bfloat16 [64, 64, 4096], P('filt', 'depth'), may hold values from -6 to 6
- w_three: bfloat16 [1728, 128], P(None, 'filt'), may hold values from -0.15625 to 0.15625
- w_four: bfloat16 [3456, 256], P(None, 'filt'), may hold values from -0.109375 to 0.109375
- cotangent: bfloat16 [256, 16, 256], P('filt', 'depth'), may hold values from -384 to 384
Outputs:
- x_grad: float32 [64, 64, 4096], P('filt', 'depth')
- w3_grad: float32 [1728, 128], P(None, 'filt')
- w4_grad: float32 [3456, 256], P(None, 'filt')
The draws below stay inside these ranges and needn't reach their ends.
All inputs are finite; a program needn't handle non-finite values.
Results may differ from the reference program's by a relative error of at most 0.014.
Values may be sent and summed in bfloat16 or wider, within the bound.
No kernel may reach another device: no remote copies, remote signals or barrier semaphores. Data moves between devices by JAX's collectives and lax.ppermute only.
A program may use at most 192 MiB of HBM per device.

```python
import math
import jax
import jax.numpy as jnp
from jax import lax

C0 = 64
C1 = 128
C2 = 256
HH = 32
WW = 128
NDEP = 64


def levels(key, shape, cuts, low, largest):
    def one(position, blocks):
        draws = jax.random.uniform(jax.random.fold_in(jax.random.fold_in(key, 6), position), (blocks,), jnp.float32, low / len(cuts), largest / len(cuts))
        return jnp.repeat(jnp.exp(draws), shape[position] // blocks).reshape((-1,) + (1,) * (len(shape) - position - 1))

    gain = one(*cuts[0])
    for cut in cuts[1:]:
        gain = gain * one(*cut)
    return gain


def centred(key, dims, scale, limit, shards=(), held_as=jnp.bfloat16):
    values = jax.random.normal(key, dims, jnp.float32) * scale
    if len(shards) > 0:
        values = levels(key, dims, shards, -0.22, 0.18) * values
    return jnp.clip(values, min=-limit, max=limit).astype(held_as)


def setup_inputs(seed: int = 0) -> dict:
    splits = jax.random.split(jax.random.key(seed), 5)
    return {
        "volume": centred(splits[0], (C0, NDEP, HH * WW), 1.0, 6.0, ((0, 2), (1, 16))),
        "w_three": centred(splits[1], (27 * C0, C1), (27 * C0) ** -0.5, 0.15625, ((1, 2),)),
        "w_four": centred(splits[2], (27 * C1, C2), (27 * C1) ** -0.5, 0.109375, ((1, 2),)),
        "cotangent": centred(splits[3], (C2, NDEP // 4, HH * WW // 16), 64.0, 384.0, ((0, 2), (1, 16))),
    }


def conv_full(field, kernel):
    return lax.conv_general_dilated(field[None], kernel, (1, 1, 1), [(1, 1), (1, 1), (1, 1)], dimension_numbers=('NCDHW', 'OIDHW', 'NCDHW'), precision=lax.Precision.HIGHEST)[0]

def kernel_of(matrix, inputs, outputs):
    return matrix.astype(jnp.float32).reshape(3, 3, 3, inputs, outputs).transpose(4, 3, 0, 1, 2)

def average_pool(field):
    chans, deep, tall, broad = field.shape
    return field.reshape(chans, deep // 2, 2, tall // 2, 2, broad // 2, 2).mean(axis=(2, 4, 6))

def spread_back(field):
    return jnp.repeat(jnp.repeat(jnp.repeat(field, 2, 1), 2, 2), 2, 3) / 8.0

def silu_slope(value):
    sigma = jax.nn.sigmoid(value)
    return sigma * (1.0 + value * (1.0 - sigma))

def reference(volume, w_three, w_four, cotangent):
    field = volume.astype(jnp.float32).reshape(C0, NDEP, HH, WW)
    kernel_three = kernel_of(w_three, C0, C1)
    kernel_four = kernel_of(w_four, C1, C2)
    pre_three = conv_full(field, kernel_three)
    pooled = average_pool(jax.nn.silu(pre_three)).astype(jnp.bfloat16)
    pooled_wide = pooled.astype(jnp.float32)
    pre_four, back_four = jax.vjp(conv_full, pooled_wide, kernel_four)
    upper = cotangent.astype(jnp.float32).reshape(C2, NDEP // 4, HH // 4, WW // 4)
    grad_four = (spread_back(upper) * silu_slope(pre_four)).astype(jnp.bfloat16)
    pooled_grad, kernel_grad_four = back_four(grad_four.astype(jnp.float32))
    scale_four = 1.0 / math.sqrt(NDEP * HH * WW / 8.0)
    w4_grad = kernel_grad_four.transpose(2, 3, 4, 1, 0).reshape(27 * C1, C2) * scale_four
    grad_three = (spread_back(pooled_grad) * silu_slope(pre_three)).astype(jnp.bfloat16)
    ignored, back_three = jax.vjp(conv_full, field, kernel_three)
    field_grad, kernel_grad_three = back_three(grad_three.astype(jnp.float32))
    scale_three = 1.0 / math.sqrt(NDEP * HH * WW * 1.0)
    w3_grad = kernel_grad_three.transpose(2, 3, 4, 1, 0).reshape(27 * C0, C1) * scale_three
    x_grad = field_grad.reshape(C0, NDEP, HH * WW)
    return (x_grad, w3_grad, w4_grad)
```

```python
import functools
import math

import jax
import jax.numpy as jnp
import numpy as np
from jax import lax
from jax.experimental import pallas as pl
from jax.experimental.pallas import tpu as pltpu
from jax.sharding import PartitionSpec as P

HH = 32
WW = 128
LANES = 128
BF = jnp.bfloat16
F32 = jnp.float32
VMEM_LIMIT = 56 * 2**20
TILES = HH // 4


def nn(a, b):
    return jnp.dot(a, b, preferred_element_type=F32)


def nt(a, b):
    return lax.dot_general(a, b, (((1,), (1,)), ((), ())), preferred_element_type=F32)


def call(body, outs, name, scratch=(), scalars=0, inputs=0):
    specs = [pl.BlockSpec(memory_space=pltpu.SMEM)] * scalars
    specs += [pl.BlockSpec(memory_space=pltpu.VMEM)] * inputs
    return pl.pallas_call(
        body,
        out_shape=[jax.ShapeDtypeStruct(shape, dtype) for shape, dtype in outs],
        in_specs=specs,
        out_specs=[pl.BlockSpec(memory_space=pltpu.VMEM)] * len(outs),
        scratch_shapes=list(scratch),
        compiler_params=pltpu.CompilerParams(vmem_limit_bytes=VMEM_LIMIT),
        name=name,
    )


def sigmoid(value):
    return 0.5 * jnp.tanh(0.5 * value) + 0.5


def shifted(block, width):
    wide = block.astype(F32)
    lane = lax.broadcasted_iota(jnp.int32, wide.shape, 1) % width
    before = jnp.where(lane == 0, 0.0, pltpu.roll(wide, 1, axis=1)).astype(BF)
    after = jnp.where(lane == width - 1, 0.0, pltpu.roll(wide, LANES - 1, axis=1)).astype(BF)
    return before, after


def fine_rows(source, windows, plane, offset, chans, group, first, count):
    def row(step, _):
        block = source(step)
        before, after = shifted(block, WW)
        lanes = pl.ds(pl.multiple_of((step - first + 1) * LANES, LANES), LANES)
        for shift, value in enumerate((before, block, after)):
            windows[plane, pl.ds(pl.multiple_of(shift * group + offset, 32), chans), lanes] = value
        return 0

    lower = max(first - 1, 0)
    upper = min(first + count + 1, HH)
    zero = jnp.zeros((chans, LANES), BF)
    for shift in range(3):
        rows = pl.ds(pl.multiple_of(shift * group + offset, 32), chans)
        if first == 0:
            windows[plane, rows, 0:LANES] = zero
        if first + count == HH:
            windows[plane, rows, (count + 1) * LANES : (count + 2) * LANES] = zero
    lax.fori_loop(lower, upper, row, 0, unroll=2)


def row_of(ref):
    def source(step):
        return ref[:, pl.ds(pl.multiple_of(step * LANES, LANES), LANES)]

    return source


def coarse_rows(source, windows, plane, offset, chans, group):
    half = LANES // 2
    lane = lax.broadcasted_iota(jnp.int32, (chans, LANES), 1)

    def put(shift, tile, value):
        rows = pl.ds(pl.multiple_of(shift * group + offset, 32), chans)
        windows[plane, rows, tile * LANES : (tile + 1) * LANES] = value

    for tile in range(TILES):
        block = source(tile)
        before, after = shifted(block, half)
        for shift, value in enumerate((before, block, after)):
            put(shift, tile + 1, value)
            if tile == 0 or tile == TILES - 1:
                turned = pltpu.roll(value.astype(F32), half, axis=1)
                if tile == TILES - 1:
                    put(shift, 0, jnp.where(lane < half, 0.0, turned).astype(BF))
                else:
                    put(shift, TILES + 1, jnp.where(lane < half, turned, 0.0).astype(BF))


def tile_of(ref):
    def source(tile):
        return ref[:, tile * LANES : (tile + 1) * LANES]

    return source


def window_planes(refs, own):
    own_ref, low, high, edge, middle, peer_low, peer_high = refs
    planes = own_ref.shape[0]
    out = [(0, low, True), (planes + 1, high, True)]
    out += [(d + 1, own_ref.at[d], True) for d in range(planes)]
    out += [(0, peer_low, False), (planes + 1, peer_high, False)]
    out += [(1, edge.at[0], False), (planes, edge.at[1], False)]
    out += [(d + 2, middle.at[d], False) for d in range(planes - 2)]
    return out


def forward_fine_kernel(filt, own, low, high, edge, middle, plow, phigh, weights, pool, pooled, slope, windows):
    chans = own.shape[1]
    planes = own.shape[0]
    mine = pl.multiple_of(filt[0] * chans, 32)
    theirs = pl.multiple_of((1 - filt[0]) * chans, 32)
    for plane, ref, is_own in window_planes((own, low, high, edge, middle, plow, phigh), True):
        fine_rows(row_of(ref), windows, plane, mine if is_own else theirs, chans, 2 * chans, 0, HH)
    outs = weights.shape[1] // 3
    span = 2 * LANES

    def chunk(j, _):
        tops = (j * 2, HH // 2 + j * 2)
        acts = []
        for d in range(planes):
            acts.append([None, None])
        for side, top in enumerate(tops):
            totals = [None] * planes
            for p in range(planes + 2):
                value = None
                for kh in range(3):
                    lanes = pl.ds(pl.multiple_of((top + kh) * LANES, LANES), span)
                    part = nn(weights[kh], windows[p, :, lanes])
                    value = part if value is None else value + part
                for kd in range(3):
                    d = p - kd
                    if 0 <= d < planes:
                        piece = value[kd * outs : (kd + 1) * outs]
                        totals[d] = piece if totals[d] is None else totals[d] + piece
            for d in range(planes):
                pre = totals[d]
                sigma = sigmoid(pre)
                act = pre * sigma
                slope[d, :, pl.ds(pl.multiple_of(top * LANES, LANES), span)] = (
                    sigma + act * (1.0 - sigma)
                ).astype(BF)
                acts[d][side] = act[:, :LANES] + act[:, LANES:]
        for d in range(0, planes, 2):
            both = jnp.concatenate(
                [acts[d][0] + acts[d + 1][0], acts[d][1] + acts[d + 1][1]], axis=1
            )
            coarse = both.astype(BF)
            rest = (both - coarse.astype(F32)).astype(BF)
            mean = nn(coarse, pool[...]) + nn(rest, pool[...])
            pooled[d // 2, :, pl.ds(pl.multiple_of(j * LANES, LANES), LANES)] = mean.astype(BF)
        return 0

    lax.fori_loop(0, TILES, chunk, 0)


def forward_coarse_kernel(filt, own, low, high, peer, plow, phigh, weights, cot, spread, grads, windows):
    planes, chans, cells = own.shape
    mine = pl.multiple_of(filt[0] * chans, 32)
    theirs = pl.multiple_of((1 - filt[0]) * chans, 32)
    sides = ((mine, low, own, high), (theirs, plow, peer, phigh))
    for offset, below, middle, above in sides:
        refs = [below] + [middle.at[d] for d in range(planes)] + [above]
        for plane, ref in enumerate(refs):
            coarse_rows(tile_of(ref), windows, plane, offset, chans, 2 * chans)
    upper = nn(cot[...], spread[...])
    span = cells // 2
    for d in range(planes):
        for start in range(0, cells, span):
            pre = None
            for kd in range(3):
                for kh in range(3):
                    begin = start + kh * LANES
                    part = nn(weights[kd * 3 + kh], windows[d + kd, :, begin : begin + span])
                    pre = part if pre is None else pre + part
            sigma = sigmoid(pre)
            slope = sigma * (1.0 + pre * (1.0 - sigma))
            grads[d, :, start : start + span] = (upper[:, start : start + span] * slope).astype(BF)


def kernel_grad_coarse_kernel(windows, grads, out, total):
    deep, group, _ = windows.shape
    planes = deep - 2
    outs = grads.shape[0] // planes
    cells = grads.shape[1]
    seen = set()
    for p in range(deep):
        first, last = max(p - 2, 0), min(p, planes - 1)
        for kh in range(3):
            value = nt(
                windows[p, :, kh * LANES : kh * LANES + cells],
                grads[first * outs : (last + 1) * outs, :],
            )
            for d in range(first, last + 1):
                index = (p - d) * 3 + kh
                rows = slice(index * group, (index + 1) * group)
                part = value[:, (d - first) * outs : (d - first + 1) * outs]
                total[rows, :] = total[rows, :] + part if index in seen else part
                seen.add(index)
    out[...] = total[...].astype(out.dtype)


def backward_coarse_kernel(grads, low, high, weights, own, peer, windows):
    planes, chans, cells = grads.shape
    refs = [low] + [grads.at[d] for d in range(planes)] + [high]
    for plane, ref in enumerate(refs):
        coarse_rows(tile_of(ref), windows, plane, 0, chans, chans)
    half = weights.shape[1] // 2
    span = cells // 2
    for d in range(planes):
        for start in range(0, cells, span):
            value = None
            for kd in range(3):
                for kh in range(3):
                    begin = start + kh * LANES
                    part = nn(weights[kd * 3 + kh], windows[d + kd, :, begin : begin + span])
                    value = part if value is None else value + part
            own[d, :, start : start + span] = value[:half]
            peer[d, :, start : start + span] = value[half:].astype(BF)


def grad_fine_kernel(own, peer, slope, unpool, grads):
    planes = own.shape[0]
    for d in range(planes):
        for j in range(TILES):
            lanes = slice(j * LANES, (j + 1) * LANES)
            block = (own[d, :, lanes] + peer[d, :, lanes].astype(F32)).astype(BF)
            wide = nn(block, unpool[...])
            for side in range(2):
                part = wide[:, side * LANES : (side + 1) * LANES]
                for a in range(2):
                    for row in (side * HH // 2 + 2 * j, side * HH // 2 + 2 * j + 1):
                        cells = slice(row * LANES, (row + 1) * LANES)
                        grads[2 * d + a, :, cells] = (
                            part * slope[2 * d + a, :, cells].astype(F32)
                        ).astype(BF)


def kernel_grad_fine_kernel(filt, own, low, high, edge, middle, plow, phigh, grads, out, windows, total):
    planes, chans, cells = own.shape
    mine = pl.multiple_of(filt[0] * chans, 32)
    theirs = pl.multiple_of((1 - filt[0]) * chans, 32)
    for plane, ref, is_own in window_planes((own, low, high, edge, middle, plow, phigh), True):
        fine_rows(row_of(ref), windows, plane, mine if is_own else theirs, chans, 2 * chans, 0, HH)
    group = windows.shape[1]
    outs = grads.shape[0] // planes
    seen = set()
    for p in range(planes + 2):
        first, last = max(p - 2, 0), min(p, planes - 1)
        for kh in range(3):
            value = nt(
                windows[p, :, kh * LANES : kh * LANES + cells],
                grads[first * outs : (last + 1) * outs, :],
            )
            for d in range(first, last + 1):
                index = (p - d) * 3 + kh
                rows = slice(index * group, (index + 1) * group)
                part = value[:, (d - first) * outs : (d - first + 1) * outs]
                total[rows, :] = total[rows, :] + part if index in seen else part
                seen.add(index)
    out[...] = total[...].astype(out.dtype)


def backward_fine_kernel(first, count, grads, low, high, weights, own, peer, windows):
    planes, chans, _ = grads.shape
    refs = [low] + [grads.at[d] for d in range(planes)] + [high]
    for plane, ref in enumerate(refs):
        fine_rows(row_of(ref), windows, plane, 0, chans, chans, first, count)
    outs = weights.shape[1] // 3
    half = outs // 2
    span = 2 * LANES

    def chunk(j, _):
        totals = [None] * planes
        for p in range(planes + 2):
            value = None
            for kh in range(3):
                lanes = pl.ds(pl.multiple_of((2 * j + kh) * LANES, LANES), span)
                part = nn(weights[kh], windows[p, :, lanes])
                value = part if value is None else value + part
            for kd in range(3):
                d = p - kd
                if 0 <= d < planes:
                    piece = value[kd * outs : (kd + 1) * outs]
                    totals[d] = piece if totals[d] is None else totals[d] + piece
        cells = pl.ds(pl.multiple_of(j * span, span), span)
        for d in range(planes):
            own[d, :, cells] = totals[d][:half]
            peer[d, :, cells] = totals[d][half:].astype(BF)
        return 0

    lax.fori_loop(0, count // 2, chunk, 0)


def to_next(value):
    count = lax.axis_size("depth")
    return lax.ppermute(value, "depth", [(i, i + 1) for i in range(count - 1)])


def to_previous(value):
    count = lax.axis_size("depth")
    return lax.ppermute(value, "depth", [(i + 1, i) for i in range(count - 1)])


def swap(value):
    return lax.ppermute(value, "filt", [(0, 1), (1, 0)])


def sum_over_depth(value):
    count = lax.axis_size("depth")
    place = lax.axis_index("depth")
    bits = [1 << k for k in range(count.bit_length() - 1)]
    rows = value.shape[0]
    value = jnp.pad(value, ((0, -rows % (8 * count)), (0, 0)))
    for bit in bits:
        half = value.shape[0] // 2
        upper = (place & bit) != 0
        keep = jnp.where(upper, value[half:], value[:half])
        send = jnp.where(upper, value[:half], value[half:])
        other = lax.ppermute(send, "depth", [(i, i ^ bit) for i in range(count)])
        value = (keep.astype(F32) + other.astype(F32)).astype(value.dtype)
    for bit in reversed(bits):
        upper = (place & bit) != 0
        other = lax.ppermute(value, "depth", [(i, i ^ bit) for i in range(count)])
        value = jnp.concatenate(
            [jnp.where(upper, other, value), jnp.where(upper, value, other)], axis=0
        )
    return value[:rows]


def pool_matrix():
    lane = np.arange(2 * LANES)
    column = np.where(lane < LANES, lane // 2, LANES // 2 + (lane - LANES) // 2)
    return (np.arange(LANES)[None] == column[:, None]) * np.float32(0.125)


def spread_matrix(tall, broad):
    lane = np.arange(4 * tall * broad)
    tile, half, w = lane // LANES, lane % LANES // (2 * broad), lane % (2 * broad)
    row = tile + half * TILES
    cell = row // 2 * broad + w // 2
    return (np.arange(tall * broad)[:, None] == cell[None]) * np.float32(0.125)


def body(volume, w_three, w_four, cotangent):
    own_in, planes, cells = volume.shape
    mid = w_three.shape[1]
    c_mid = w_four.shape[0] // 27
    outs = w_four.shape[1]
    half_planes = planes // 2
    coarse = cells // 4
    filt = lax.axis_index("filt")
    which = filt.astype(jnp.int32).reshape(1)

    own = volume.transpose(1, 0, 2)
    edge = swap(jnp.stack([own[0], own[planes - 1]]))
    middle = swap(own[1 : planes - 1])
    low, high = to_next(own[planes - 1]), to_previous(own[0])
    plow, phigh = to_next(edge[1]), to_previous(edge[0])

    fine = w_three.reshape(3, 3, 3, 2 * own_in, mid)
    fine_forward = fine.transpose(1, 0, 4, 2, 3).reshape(3, 3 * mid, 6 * own_in)
    turned = fine[::-1, ::-1, ::-1].reshape(3, 3, 3, 2, own_in, mid)
    turned = jnp.where(filt == 0, turned, turned[:, :, :, ::-1])
    fine_backward = turned.transpose(1, 0, 3, 4, 2, 5).reshape(3, 6 * own_in, 3 * mid)
    wide = w_four.reshape(3, 3, 3, c_mid, outs)
    wide_forward = wide.transpose(0, 1, 4, 2, 3).reshape(9, outs, 3 * c_mid)
    turned = wide[::-1, ::-1, ::-1].reshape(3, 3, 3, 2, mid, outs)
    turned = jnp.where(filt == 0, turned, turned[:, :, :, ::-1])
    wide_backward = turned.transpose(0, 1, 3, 4, 2, 5).reshape(9, c_mid, 3 * outs)
    pool = jnp.asarray(pool_matrix(), BF)
    unpool = jnp.asarray(pool_matrix().T, BF)
    spread = jnp.asarray(spread_matrix(HH // 4, WW // 4), BF)

    fine_windows = pltpu.VMEM((planes + 2, 6 * own_in, (HH + 2) * LANES), BF)
    pooled, slope = call(
        forward_fine_kernel,
        [((half_planes, mid, coarse), BF), ((planes, mid, cells), BF)],
        "forward_fine",
        [fine_windows],
        scalars=1,
        inputs=9,
    )(which, own, low, high, edge, middle, plow, phigh, fine_forward, pool)

    pooled_peer = swap(pooled)
    pool_low, pool_high = to_next(pooled[half_planes - 1]), to_previous(pooled[0])
    ppool_low, ppool_high = to_next(pooled_peer[half_planes - 1]), to_previous(pooled_peer[0])
    coarse_lanes = (TILES + 2) * LANES
    grad_four, coarse_windows = call(
        forward_coarse_kernel,
        [
            ((half_planes, outs, coarse), BF),
            ((half_planes + 2, 3 * c_mid, coarse_lanes), BF),
        ],
        "forward_coarse",
        scalars=1,
        inputs=9,
    )(
        which,
        pooled,
        pool_low,
        pool_high,
        pooled_peer,
        ppool_low,
        ppool_high,
        wide_forward,
        cotangent.reshape(outs, -1),
        spread,
    )

    four_low, four_high = to_next(grad_four[half_planes - 1]), to_previous(grad_four[0])
    (coarse_kernel,) = call(
        kernel_grad_coarse_kernel,
        [((27 * c_mid, outs), BF)],
        "kernel_grad_coarse",
        [pltpu.VMEM((27 * c_mid, outs), F32)],
        inputs=2,
    )(coarse_windows, grad_four.reshape(half_planes * outs, coarse))
    own_back, peer_back = call(
        backward_coarse_kernel,
        [((half_planes, mid, coarse), F32), ((half_planes, mid, coarse), BF)],
        "backward_coarse",
        [pltpu.VMEM((half_planes + 2, 3 * outs, coarse_lanes), BF)],
        inputs=4,
    )(grad_four, four_low, four_high, wide_backward)
    peer_back = swap(peer_back)
    coarse_sum = sum_over_depth(coarse_kernel)

    (grad_three,) = call(
        grad_fine_kernel, [((planes, mid, cells), BF)], "grad_fine", inputs=4
    )(own_back, peer_back, slope, unpool)
    three_low, three_high = to_next(grad_three[planes - 1]), to_previous(grad_three[0])
    (fine_kernel,) = call(
        kernel_grad_fine_kernel,
        [((54 * own_in, mid), BF)],
        "kernel_grad_fine",
        [fine_windows, pltpu.VMEM((54 * own_in, mid), F32)],
        scalars=1,
        inputs=8,
    )(which, own, low, high, edge, middle, plow, phigh, grad_three.reshape(planes * mid, cells))
    fine_sum = sum_over_depth(fine_kernel.reshape(27 * own_in, 2 * mid)).reshape(54 * own_in, mid)

    parts = 2
    count = HH // parts
    owns, peers = [], []
    for part in range(parts):
        mine, theirs = call(
            functools.partial(backward_fine_kernel, part * count, count),
            [((planes, own_in, count * WW), F32), ((planes, own_in, count * WW), BF)],
            f"backward_fine_{part}",
            [pltpu.VMEM((planes + 2, 3 * mid, (count + 2) * LANES), BF)],
            inputs=4,
        )(grad_three, three_low, three_high, fine_backward)
        owns.append(mine)
        peers.append(swap(theirs))
    x_grad = jnp.concatenate([a + b.astype(F32) for a, b in zip(owns, peers)], axis=2)
    x_grad = x_grad.transpose(1, 0, 2)

    all_cells = planes * lax.axis_size("depth") * cells
    scale_four = 1.0 / math.sqrt(all_cells / 8.0)
    scale_three = 1.0 / math.sqrt(all_cells * 1.0)
    return (x_grad, fine_sum.astype(F32) * scale_three, coarse_sum.astype(F32) * scale_four)


def solution(mesh):
    return jax.shard_map(
        body,
        mesh=mesh,
        in_specs=(
            P("filt", "depth", None),
            P(None, "filt"),
            P(None, "filt"),
            P("filt", "depth", None),
        ),
        out_specs=(P("filt", "depth", None), P(None, "filt"), P(None, "filt")),
        check_vma=False,
    )
```

```python
import functools
import math

import jax
import jax.numpy as jnp
import numpy as np
from jax import lax
from jax.experimental import pallas as pl
from jax.experimental.pallas import tpu as pltpu
from jax.sharding import PartitionSpec as P

HH = 32
WW = 128
LANES = 128
BF = jnp.bfloat16
F32 = jnp.float32
VMEM_LIMIT = 56 * 2**20
TILES = HH // 4


def nn(a, b):
    return jnp.dot(a, b, preferred_element_type=F32)


def nt(a, b):
    return lax.dot_general(a, b, (((1,), (1,)), ((), ())), preferred_element_type=F32)


def call(body, outs, name, scratch=(), scalars=0, inputs=0, gflop=1.0):
    specs = [pl.BlockSpec(memory_space=pltpu.SMEM)] * scalars
    specs += [pl.BlockSpec(memory_space=pltpu.VMEM)] * inputs
    return pl.pallas_call(
        body,
        out_shape=[jax.ShapeDtypeStruct(shape, dtype) for shape, dtype in outs],
        in_specs=specs,
        out_specs=[pl.BlockSpec(memory_space=pltpu.VMEM)] * len(outs),
        scratch_shapes=list(scratch),
        compiler_params=pltpu.CompilerParams(vmem_limit_bytes=VMEM_LIMIT),
        cost_estimate=pl.CostEstimate(
            flops=int(gflop * 1e9), transcendentals=0, bytes_accessed=4 * 2**20
        ),
        name=name,
    )


def sigmoid(value):
    return 0.5 * jnp.tanh(0.5 * value) + 0.5


def shifted(block, width):
    lane = lax.broadcasted_iota(jnp.int32, block.shape, 1) % width
    zero = jnp.zeros(block.shape, BF)
    before = jnp.where(lane == 0, zero, pltpu.roll(block, 1, axis=1))
    after = jnp.where(lane == width - 1, zero, pltpu.roll(block, LANES - 1, axis=1))
    return before, after


def fine_rows(source, windows, plane, offset, chans, group, first, count):
    def row(step, _):
        block = source(step)
        before, after = shifted(block, WW)
        lanes = pl.ds(pl.multiple_of((step - first + 1) * LANES, LANES), LANES)
        for shift, value in enumerate((before, block, after)):
            windows[plane, pl.ds(pl.multiple_of(shift * group + offset, 32), chans), lanes] = value
        return 0

    lower = max(first - 1, 0)
    upper = min(first + count + 1, HH)
    zero = jnp.zeros((chans, LANES), BF)
    for shift in range(3):
        rows = pl.ds(pl.multiple_of(shift * group + offset, 32), chans)
        if first == 0:
            windows[plane, rows, 0:LANES] = zero
        if first + count == HH:
            windows[plane, rows, (count + 1) * LANES : (count + 2) * LANES] = zero
    lax.fori_loop(lower, upper, row, 0, unroll=16)


def row_of(ref):
    def source(step):
        return ref[:, pl.ds(pl.multiple_of(step * LANES, LANES), LANES)]

    return source


def coarse_rows(source, windows, plane, offset, chans, group):
    half = LANES // 2
    lane = lax.broadcasted_iota(jnp.int32, (chans, LANES), 1)

    def put(shift, tile, value):
        rows = pl.ds(pl.multiple_of(shift * group + offset, 32), chans)
        windows[plane, rows, tile * LANES : (tile + 1) * LANES] = value

    for tile in range(TILES):
        block = source(tile)
        before, after = shifted(block, half)
        for shift, value in enumerate((before, block, after)):
            put(shift, tile + 1, value)
            if tile == 0 or tile == TILES - 1:
                turned = pltpu.roll(value.astype(F32), half, axis=1)
                if tile == TILES - 1:
                    put(shift, 0, jnp.where(lane < half, 0.0, turned).astype(BF))
                else:
                    put(shift, TILES + 1, jnp.where(lane < half, turned, 0.0).astype(BF))


def tile_of(ref):
    def source(tile):
        return ref[:, tile * LANES : (tile + 1) * LANES]

    return source


def window_planes(refs, own):
    own_ref, low, high, edge, middle, peer_low, peer_high = refs
    planes = own_ref.shape[0]
    out = [(0, low, True), (planes + 1, high, True)]
    out += [(d + 1, own_ref.at[d], True) for d in range(planes)]
    out += [(0, peer_low, False), (planes + 1, peer_high, False)]
    out += [(1, edge.at[0], False), (planes, edge.at[1], False)]
    out += [(d + 2, middle.at[d], False) for d in range(planes - 2)]
    return out


def forward_fine_kernel(filt, own, low, high, edge, middle, plow, phigh, weights, pool, pooled, slope, windows):
    chans = own.shape[1]
    planes = own.shape[0]
    mine = pl.multiple_of(filt[0] * chans, 32)
    theirs = pl.multiple_of((1 - filt[0]) * chans, 32)
    for plane, ref, is_own in window_planes((own, low, high, edge, middle, plow, phigh), True):
        fine_rows(row_of(ref), windows, plane, mine if is_own else theirs, chans, 2 * chans, 0, HH)
    outs = weights.shape[1] // 3
    span = 2 * LANES

    def chunk(j, _):
        tops = (j * 2, HH // 2 + j * 2)
        acts = []
        for d in range(planes):
            acts.append([None, None])
        for side, top in enumerate(tops):
            totals = [None] * planes
            for p in range(planes + 2):
                value = None
                for kh in range(3):
                    lanes = pl.ds(pl.multiple_of((top + kh) * LANES, LANES), span)
                    part = nn(weights[kh], windows[p, :, lanes])
                    value = part if value is None else value + part
                for kd in range(3):
                    d = p - kd
                    if 0 <= d < planes:
                        piece = value[kd * outs : (kd + 1) * outs]
                        totals[d] = piece if totals[d] is None else totals[d] + piece
            for d in range(planes):
                pre = totals[d]
                sigma = sigmoid(pre)
                act = pre * sigma
                slope[d, :, pl.ds(pl.multiple_of(top * LANES, LANES), span)] = (
                    sigma + act * (1.0 - sigma)
                ).astype(BF)
                acts[d][side] = act[:, :LANES] + act[:, LANES:]
        for d in range(0, planes, 2):
            both = jnp.concatenate(
                [acts[d][0] + acts[d + 1][0], acts[d][1] + acts[d + 1][1]], axis=1
            )
            coarse = both.astype(BF)
            rest = (both - coarse.astype(F32)).astype(BF)
            mean = nn(coarse, pool[...]) + nn(rest, pool[...])
            pooled[d // 2, :, pl.ds(pl.multiple_of(j * LANES, LANES), LANES)] = mean.astype(BF)
        return 0

    lax.fori_loop(0, TILES, chunk, 0, unroll=4)


def forward_coarse_kernel(filt, own, peer, low, high, weights, cot, spread, grads, windows, first_out, last_out):
    planes, chans, cells = own.shape
    mine = pl.multiple_of(filt[0] * chans, 32)
    theirs = pl.multiple_of((1 - filt[0]) * chans, 32)
    sides = ((mine, low.at[0], own, high.at[0]), (theirs, low.at[1], peer, high.at[1]))
    for offset, below, middle, above in sides:
        refs = [below] + [middle.at[d] for d in range(planes)] + [above]
        for plane, ref in enumerate(refs):
            coarse_rows(tile_of(ref), windows, plane, offset, chans, 2 * chans)
    upper = nn(cot[...], spread[...])
    span = cells // 2
    for d in range(planes):
        for start in range(0, cells, span):
            pre = None
            for kd in range(3):
                for kh in range(3):
                    begin = start + kh * LANES
                    part = nn(weights[kd * 3 + kh], windows[d + kd, :, begin : begin + span])
                    pre = part if pre is None else pre + part
            sigma = sigmoid(pre)
            slope = sigma * (1.0 + pre * (1.0 - sigma))
            value = (upper[:, start : start + span] * slope).astype(BF)
            grads[d, :, start : start + span] = value
            if d == 0:
                first_out[:, start : start + span] = value
            if d == planes - 1:
                last_out[:, start : start + span] = value


def kernel_grad_coarse_kernel(windows, grads, out, total):
    deep, group, _ = windows.shape
    planes = deep - 2
    outs = grads.shape[0] // planes
    cells = grads.shape[1]
    seen = set()
    for p in range(deep):
        first, last = max(p - 2, 0), min(p, planes - 1)
        for kh in range(3):
            value = nt(
                windows[p, :, kh * LANES : kh * LANES + cells],
                grads[first * outs : (last + 1) * outs, :],
            )
            for d in range(first, last + 1):
                index = (p - d) * 3 + kh
                rows = slice(index * group, (index + 1) * group)
                part = value[:, (d - first) * outs : (d - first + 1) * outs]
                total[rows, :] = total[rows, :] + part if index in seen else part
                seen.add(index)
    out[...] = total[...].astype(out.dtype)


def backward_coarse_kernel(grads, low, high, weights, own, peer, windows):
    planes, chans, cells = grads.shape
    refs = [low] + [grads.at[d] for d in range(planes)] + [high]
    for plane, ref in enumerate(refs):
        coarse_rows(tile_of(ref), windows, plane, 0, chans, chans)
    half = weights.shape[1] // 2
    span = cells // 2
    for d in range(planes):
        for start in range(0, cells, span):
            value = None
            for kd in range(3):
                for kh in range(3):
                    begin = start + kh * LANES
                    part = nn(weights[kd * 3 + kh], windows[d + kd, :, begin : begin + span])
                    value = part if value is None else value + part
            own[d, :, start : start + span] = value[:half]
            peer[d, :, start : start + span] = value[half:].astype(BF)


def grad_fine_kernel(own, peer, slope, unpool, grads, first_out, last_out):
    planes = own.shape[0]
    for d in range(planes):
        for j in range(TILES):
            lanes = slice(j * LANES, (j + 1) * LANES)
            block = (own[d, :, lanes] + peer[d, :, lanes].astype(F32)).astype(BF)
            wide = nn(block, unpool[...])
            for side in range(2):
                part = wide[:, side * LANES : (side + 1) * LANES]
                for a in range(2):
                    for row in (side * HH // 2 + 2 * j, side * HH // 2 + 2 * j + 1):
                        cells = slice(row * LANES, (row + 1) * LANES)
                        value = (part * slope[2 * d + a, :, cells].astype(F32)).astype(BF)
                        grads[2 * d + a, :, cells] = value
                        if 2 * d + a == 0:
                            first_out[:, cells] = value
                        if 2 * d + a == 2 * planes - 1:
                            last_out[:, cells] = value


def kernel_grad_fine_kernel(filt, own, low, high, edge, middle, plow, phigh, grads, out, windows, total):
    planes, chans, cells = own.shape
    mine = pl.multiple_of(filt[0] * chans, 32)
    theirs = pl.multiple_of((1 - filt[0]) * chans, 32)
    for plane, ref, is_own in window_planes((own, low, high, edge, middle, plow, phigh), True):
        fine_rows(row_of(ref), windows, plane, mine if is_own else theirs, chans, 2 * chans, 0, HH)
    group = windows.shape[1]
    outs = grads.shape[0] // planes
    seen = set()
    for p in range(planes + 2):
        first, last = max(p - 2, 0), min(p, planes - 1)
        for kh in range(3):
            value = nt(
                windows[p, :, kh * LANES : kh * LANES + cells],
                grads[first * outs : (last + 1) * outs, :],
            )
            for d in range(first, last + 1):
                index = (p - d) * 3 + kh
                rows = slice(index * group, (index + 1) * group)
                part = value[:, (d - first) * outs : (d - first + 1) * outs]
                total[rows, :] = total[rows, :] + part if index in seen else part
                seen.add(index)
    out[...] = total[...].astype(out.dtype)


def backward_fine_kernel(first, count, grads, low, high, weights, own, peer, windows):
    planes, chans, _ = grads.shape
    refs = [low] + [grads.at[d] for d in range(planes)] + [high]
    for plane, ref in enumerate(refs):
        fine_rows(row_of(ref), windows, plane, 0, chans, chans, first, count)
    outs = weights.shape[1] // 3
    half = outs // 2
    span = 2 * LANES

    def chunk(j, _):
        totals = [None] * planes
        for p in range(planes + 2):
            value = None
            for kh in range(3):
                lanes = pl.ds(pl.multiple_of((2 * j + kh) * LANES, LANES), span)
                part = nn(weights[kh], windows[p, :, lanes])
                value = part if value is None else value + part
            for kd in range(3):
                d = p - kd
                if 0 <= d < planes:
                    piece = value[kd * outs : (kd + 1) * outs]
                    totals[d] = piece if totals[d] is None else totals[d] + piece
        cells = pl.ds(pl.multiple_of(j * span, span), span)
        for d in range(planes):
            own[d, :, cells] = totals[d][:half]
            peer[d, :, cells] = totals[d][half:].astype(BF)
        return 0

    lax.fori_loop(0, count // 2, chunk, 0, unroll=4)


def to_next(value):
    count = lax.axis_size("depth")
    return lax.ppermute(value, "depth", [(i, i + 1) for i in range(count - 1)])


def to_previous(value):
    count = lax.axis_size("depth")
    return lax.ppermute(value, "depth", [(i + 1, i) for i in range(count - 1)])


def swap(value):
    return lax.ppermute(value, "filt", [(0, 1), (1, 0)])


def halves(value, bit):
    upper = (lax.axis_index("depth") & bit) != 0
    half = value.shape[0] // 2
    return (
        jnp.where(upper, value[half:], value[:half]),
        jnp.where(upper, value[:half], value[half:]),
    )


def across(value, bit):
    count = lax.axis_size("depth")
    return lax.ppermute(value, "depth", [(i, i ^ bit) for i in range(count)])


def plus(a, b):
    return (a.astype(F32) + b.astype(F32)).astype(a.dtype)


def scatter_step(value, bit):
    keep, send = halves(value, bit)
    return plus(keep, across(send, bit))


def gather_step(value, bit):
    upper = (lax.axis_index("depth") & bit) != 0
    other = across(value, bit)
    return jnp.concatenate(
        [jnp.where(upper, other, value), jnp.where(upper, value, other)], axis=0
    )


def after(value, *others):
    return lax.optimization_barrier((value, *others))[0]


def pool_matrix():
    lane = np.arange(2 * LANES)
    column = np.where(lane < LANES, lane // 2, LANES // 2 + (lane - LANES) // 2)
    return (np.arange(LANES)[None] == column[:, None]) * np.float32(0.125)


def spread_matrix(tall, broad):
    lane = np.arange(4 * tall * broad)
    tile, half, w = lane // LANES, lane % LANES // (2 * broad), lane % (2 * broad)
    row = tile + half * TILES
    cell = row // 2 * broad + w // 2
    return (np.arange(tall * broad)[:, None] == cell[None]) * np.float32(0.125)


def body(volume, w_three, w_four, cotangent):
    own_in, planes, cells = volume.shape
    mid = w_three.shape[1]
    c_mid = w_four.shape[0] // 27
    outs = w_four.shape[1]
    half_planes = planes // 2
    coarse = cells // 4
    filt = lax.axis_index("filt")
    which = filt.astype(jnp.int32).reshape(1)

    own = volume.transpose(1, 0, 2)
    edge = swap(jnp.stack([own[0], own[planes - 1]]))
    middle = swap(own[1 : planes - 1])
    low, high = to_next(own[planes - 1]), to_previous(own[0])
    plow, phigh = to_next(edge[1]), to_previous(edge[0])

    fine = w_three.reshape(3, 3, 3, 2 * own_in, mid)
    fine_forward = fine.transpose(1, 0, 4, 2, 3).reshape(3, 3 * mid, 6 * own_in)
    turned = fine[::-1, ::-1, ::-1].reshape(3, 3, 3, 2, own_in, mid)
    turned = jnp.where(filt == 0, turned, turned[:, :, :, ::-1])
    fine_backward = turned.transpose(1, 0, 3, 4, 2, 5).reshape(3, 6 * own_in, 3 * mid)
    wide = w_four.reshape(3, 3, 3, c_mid, outs)
    wide_forward = wide.transpose(0, 1, 4, 2, 3).reshape(9, outs, 3 * c_mid)
    turned = wide[::-1, ::-1, ::-1].reshape(3, 3, 3, 2, mid, outs)
    turned = jnp.where(filt == 0, turned, turned[:, :, :, ::-1])
    wide_backward = turned.transpose(0, 1, 3, 4, 2, 5).reshape(9, c_mid, 3 * outs)
    pool = jnp.asarray(pool_matrix(), BF)
    unpool = jnp.asarray(pool_matrix().T, BF)
    spread = jnp.asarray(spread_matrix(HH // 4, WW // 4), BF)

    fine_forward, fine_backward, wide_forward, wide_backward, middle = lax.optimization_barrier(
        (fine_forward, fine_backward, wide_forward, wide_backward, middle)
    )

    fine_windows = pltpu.VMEM((planes + 2, 6 * own_in, (HH + 2) * LANES), BF)
    pooled, slope = call(
        forward_fine_kernel,
        [((half_planes, mid, coarse), BF), ((planes, mid, cells), BF)],
        "forward_fine",
        [fine_windows],
        scalars=1,
        inputs=9,
        gflop=17.0,
    )(which, own, low, high, edge, middle, plow, phigh, fine_forward, pool)

    pooled_peer = swap(pooled)
    pool_low = to_next(jnp.stack([pooled[half_planes - 1], pooled_peer[half_planes - 1]]))
    pool_high = to_previous(jnp.stack([pooled[0], pooled_peer[0]]))
    coarse_lanes = (TILES + 2) * LANES
    grad_four, coarse_windows, four_first, four_last = call(
        forward_coarse_kernel,
        [
            ((half_planes, outs, coarse), BF),
            ((half_planes + 2, 3 * c_mid, coarse_lanes), BF),
            ((outs, coarse), BF),
            ((outs, coarse), BF),
        ],
        "forward_coarse",
        scalars=1,
        inputs=7,
        gflop=6.0,
    )(
        which,
        pooled,
        pooled_peer,
        pool_low,
        pool_high,
        wide_forward,
        cotangent.reshape(outs, -1),
        spread,
    )

    four_low, four_high = to_next(four_last), to_previous(four_first)
    (coarse_kernel,) = call(
        kernel_grad_coarse_kernel,
        [((27 * c_mid, outs), BF)],
        "kernel_grad_coarse",
        [pltpu.VMEM((27 * c_mid, outs), F32)],
        inputs=2,
        gflop=6.0,
    )(coarse_windows, grad_four.reshape(half_planes * outs, coarse))
    own_back, peer_back = call(
        backward_coarse_kernel,
        [((half_planes, mid, coarse), F32), ((half_planes, mid, coarse), BF)],
        "backward_coarse",
        [pltpu.VMEM((half_planes + 2, 3 * outs, coarse_lanes), BF)],
        inputs=4,
        gflop=5.0,
    )(after(grad_four, coarse_kernel), four_low, four_high, wide_backward)
    peer_back = swap(peer_back)
    count = lax.axis_size("depth")
    coarse_sum = scatter_step(scatter_step(coarse_kernel, 1), 2)
    groups = [[k + 4 * m for m in range(count // 4)] for k in range(4)]
    coarse_sum = lax.psum(coarse_sum.astype(F32), "depth", axis_index_groups=groups).astype(BF)

    grad_three, three_first, three_last = call(
        grad_fine_kernel,
        [((planes, mid, cells), BF), ((mid, cells), BF), ((mid, cells), BF)],
        "grad_fine",
        inputs=4,
        gflop=3.0,
    )(own_back, peer_back, slope, unpool)
    three_low, three_high = to_next(three_last), to_previous(three_first)
    (fine_kernel,) = call(
        kernel_grad_fine_kernel,
        [((54 * own_in, mid), BF)],
        "kernel_grad_fine",
        [fine_windows, pltpu.VMEM((54 * own_in, mid), F32)],
        scalars=1,
        inputs=8,
        gflop=15.0,
    )(which, own, low, high, edge, middle, plow, phigh, grad_three.reshape(planes * mid, cells))

    fine_sum = fine_kernel.reshape(27 * own_in, 2 * mid)
    fine_sum = jnp.pad(fine_sum, ((0, -fine_sum.shape[0] % 64), (0, 0)))
    steps = [(1, scatter_step), (2, scatter_step)]
    bit = 4
    while bit < count:
        steps.append((bit, lambda v, bit: plus(v, across(v, bit))))
        bit *= 2
    steps += [(2, gather_step), (1, gather_step)]

    parts = 4
    rows = HH // parts
    owns, peers = [], []
    source = after(grad_three, fine_kernel)
    for part in range(parts):
        mine, theirs = call(
            functools.partial(backward_fine_kernel, part * rows, rows),
            [((planes, own_in, rows * WW), F32), ((planes, own_in, rows * WW), BF)],
            f"backward_fine_{part}",
            [pltpu.VMEM((planes + 2, 3 * mid, (rows + 2) * LANES), BF)],
            inputs=4,
            gflop=5.0,
        )(source, three_low, three_high, fine_backward)
        owns.append(mine)
        peers.append(swap(theirs))
        bit, step = steps.pop(0)
        fine_sum = step(fine_sum, bit)
        source = after(source, fine_sum, mine)
    for bit, step in steps:
        fine_sum = step(fine_sum, bit)
    fine_sum = fine_sum[: 27 * own_in].reshape(54 * own_in, mid)
    coarse_sum = gather_step(gather_step(coarse_sum, 2), 1)
    x_grad = jnp.concatenate([a + b.astype(F32) for a, b in zip(owns, peers)], axis=2)
    x_grad = x_grad.transpose(1, 0, 2)

    all_cells = planes * lax.axis_size("depth") * cells
    scale_four = 1.0 / math.sqrt(all_cells / 8.0)
    scale_three = 1.0 / math.sqrt(all_cells * 1.0)
    return (x_grad, fine_sum.astype(F32) * scale_three, coarse_sum.astype(F32) * scale_four)


def solution(mesh):
    return jax.shard_map(
        body,
        mesh=mesh,
        in_specs=(
            P("filt", "depth", None),
            P(None, "filt"),
            P(None, "filt"),
            P("filt", "depth", None),
        ),
        out_specs=(P("filt", "depth", None), P(None, "filt"), P(None, "filt")),
        check_vma=False,
    )
```

```python
import functools
import math

import jax
import jax.numpy as jnp
import numpy as np
from jax import lax
from jax.experimental import pallas as pl
from jax.experimental.pallas import tpu as pltpu
from jax.sharding import PartitionSpec as P

HH = 32
WW = 128
LANES = 128
BF = jnp.bfloat16
F32 = jnp.float32
VMEM_LIMIT = 28 * 2**20
TILES = HH // 4
ROWS = 16


def nn(a, b):
    return jnp.dot(a, b, preferred_element_type=F32)


def nt(a, b):
    return lax.dot_general(a, b, (((1,), (1,)), ((), ())), preferred_element_type=F32)


def call(body, outs, name, scratch=(), scalars=0, inputs=0, gflop=1.0):
    specs = [pl.BlockSpec(memory_space=pltpu.SMEM)] * scalars
    specs += [pl.BlockSpec(memory_space=pltpu.VMEM)] * inputs
    return pl.pallas_call(
        body,
        out_shape=[jax.ShapeDtypeStruct(shape, dtype) for shape, dtype in outs],
        in_specs=specs,
        out_specs=[pl.BlockSpec(memory_space=pltpu.VMEM)] * len(outs),
        scratch_shapes=list(scratch),
        compiler_params=pltpu.CompilerParams(vmem_limit_bytes=VMEM_LIMIT),
        cost_estimate=pl.CostEstimate(
            flops=int(gflop * 1e9), transcendentals=0, bytes_accessed=4 * 2**20
        ),
        name=name,
    )


def sigmoid(value):
    return 0.5 * jnp.tanh(0.5 * value) + 0.5


def shifted(block, width):
    lane = lax.broadcasted_iota(jnp.int32, block.shape, 1) % width
    zero = jnp.zeros(block.shape, BF)
    before = jnp.where(lane == 0, zero, pltpu.roll(block, 1, axis=1))
    after = jnp.where(lane == width - 1, zero, pltpu.roll(block, LANES - 1, axis=1))
    return before, after


def fine_rows(source, windows, plane, offset, chans, group, first, count):
    lower = max(first - 1, 0)
    upper = min(first + count + 1, HH)

    def row(step):
        block = source(step)
        before, after = shifted(block, WW)
        lanes = pl.ds(pl.multiple_of((step - first + 1) * LANES, LANES), LANES)
        for shift, value in enumerate((before, block, after)):
            windows[plane, pl.ds(pl.multiple_of(shift * group + offset, 32), chans), lanes] = value

    def several(turn, _):
        for k in range(ROWS):
            row(lower + turn * ROWS + k)
        return 0

    zero = jnp.zeros((chans, LANES), BF)
    for shift in range(3):
        rows = pl.ds(pl.multiple_of(shift * group + offset, 32), chans)
        if first == 0:
            windows[plane, rows, 0:LANES] = zero
        if first + count == HH:
            windows[plane, rows, (count + 1) * LANES : (count + 2) * LANES] = zero
    lax.fori_loop(0, (upper - lower) // ROWS, several, 0)
    for step in range(upper - (upper - lower) % ROWS, upper):
        row(step)


def row_of(ref):
    def source(step):
        return ref[:, pl.ds(pl.multiple_of(step * LANES, LANES), LANES)]

    return source


def coarse_rows(source, windows, plane, offset, chans, group):
    half = LANES // 2
    lane = lax.broadcasted_iota(jnp.int32, (chans, LANES), 1)

    def put(shift, tile, value):
        rows = pl.ds(pl.multiple_of(shift * group + offset, 32), chans)
        windows[plane, rows, tile * LANES : (tile + 1) * LANES] = value

    for tile in range(TILES):
        block = source(tile)
        before, after = shifted(block, half)
        for shift, value in enumerate((before, block, after)):
            put(shift, tile + 1, value)
            if tile == 0 or tile == TILES - 1:
                turned = pltpu.roll(value.astype(F32), half, axis=1)
                if tile == TILES - 1:
                    put(shift, 0, jnp.where(lane < half, 0.0, turned).astype(BF))
                else:
                    put(shift, TILES + 1, jnp.where(lane < half, turned, 0.0).astype(BF))


def tile_of(ref):
    def source(tile):
        return ref[:, tile * LANES : (tile + 1) * LANES]

    return source


def each(count, build):
    def step(d, _):
        build(d)
        return 0

    lax.fori_loop(0, count, step, 0)


def volume_windows(filt, refs, windows):
    own, low, high, edge, middle, peer_low, peer_high = refs
    planes, chans, _ = own.shape
    mine = pl.multiple_of(filt[0] * chans, 32)
    theirs = pl.multiple_of((1 - filt[0]) * chans, 32)

    def put(ref, plane, offset):
        fine_rows(row_of(ref), windows, plane, offset, chans, 2 * chans, 0, HH)

    each(planes, lambda d: put(own.at[d], d + 1, mine))
    each(planes - 2, lambda d: put(middle.at[d], d + 2, theirs))
    each(2, lambda d: put(edge.at[d], 1 + d * (planes - 1), theirs))
    put(low, 0, mine)
    put(high, planes + 1, mine)
    put(peer_low, 0, theirs)
    put(peer_high, planes + 1, theirs)


def forward_fine_kernel(filt, own, low, high, edge, middle, plow, phigh, weights, pool, pooled, slope, windows):
    planes = own.shape[0]
    volume_windows(filt, (own, low, high, edge, middle, plow, phigh), windows)
    outs = weights.shape[1] // 3
    span = 2 * LANES

    def chunk(j, _):
        tops = (j * 2, HH // 2 + j * 2)
        acts = []
        for d in range(planes):
            acts.append([None, None])
        for side, top in enumerate(tops):
            totals = [None] * planes
            for p in range(planes + 2):
                value = None
                for kh in range(3):
                    lanes = pl.ds(pl.multiple_of((top + kh) * LANES, LANES), span)
                    part = nn(weights[kh], windows[p, :, lanes])
                    value = part if value is None else value + part
                for kd in range(3):
                    d = p - kd
                    if 0 <= d < planes:
                        piece = value[kd * outs : (kd + 1) * outs]
                        totals[d] = piece if totals[d] is None else totals[d] + piece
            for d in range(planes):
                pre = totals[d]
                sigma = sigmoid(pre)
                act = pre * sigma
                slope[d, :, pl.ds(pl.multiple_of(top * LANES, LANES), span)] = (
                    sigma + act * (1.0 - sigma)
                ).astype(BF)
                acts[d][side] = act[:, :LANES] + act[:, LANES:]
        for d in range(0, planes, 2):
            both = jnp.concatenate(
                [acts[d][0] + acts[d + 1][0], acts[d][1] + acts[d + 1][1]], axis=1
            )
            coarse = both.astype(BF)
            rest = (both - coarse.astype(F32)).astype(BF)
            mean = nn(coarse, pool[...]) + nn(rest, pool[...])
            pooled[d // 2, :, pl.ds(pl.multiple_of(j * LANES, LANES), LANES)] = mean.astype(BF)
        return 0

    lax.fori_loop(0, TILES, chunk, 0, unroll=2)


def forward_coarse_kernel(filt, own, peer, low, high, weights, cot, spread, grads, windows, first_out, last_out):
    planes, chans, cells = own.shape
    mine = pl.multiple_of(filt[0] * chans, 32)
    theirs = pl.multiple_of((1 - filt[0]) * chans, 32)
    sides = ((mine, low.at[0], own, high.at[0]), (theirs, low.at[1], peer, high.at[1]))
    for offset, below, middle, above in sides:
        refs = [below] + [middle.at[d] for d in range(planes)] + [above]
        for plane, ref in enumerate(refs):
            coarse_rows(tile_of(ref), windows, plane, offset, chans, 2 * chans)
    upper = nn(cot[...], spread[...])
    span = cells // 2
    for d in range(planes):
        for start in range(0, cells, span):
            pre = None
            for kd in range(3):
                for kh in range(3):
                    begin = start + kh * LANES
                    part = nn(weights[kd * 3 + kh], windows[d + kd, :, begin : begin + span])
                    pre = part if pre is None else pre + part
            sigma = sigmoid(pre)
            slope = sigma * (1.0 + pre * (1.0 - sigma))
            value = (upper[:, start : start + span] * slope).astype(BF)
            grads[d, :, start : start + span] = value
            if d == 0:
                first_out[:, start : start + span] = value
            if d == planes - 1:
                last_out[:, start : start + span] = value


def kernel_grad_coarse_kernel(windows, grads, out, total):
    deep, group, _ = windows.shape
    planes = deep - 2
    outs = grads.shape[0] // planes
    cells = grads.shape[1]
    seen = set()
    for p in range(deep):
        first, last = max(p - 2, 0), min(p, planes - 1)
        for kh in range(3):
            value = nt(
                windows[p, :, kh * LANES : kh * LANES + cells],
                grads[first * outs : (last + 1) * outs, :],
            )
            for d in range(first, last + 1):
                index = (p - d) * 3 + kh
                rows = slice(index * group, (index + 1) * group)
                part = value[:, (d - first) * outs : (d - first + 1) * outs]
                total[rows, :] = total[rows, :] + part if index in seen else part
                seen.add(index)
    out[...] = total[...].astype(out.dtype)


def backward_coarse_kernel(grads, low, high, weights, own, peer, windows):
    planes, chans, cells = grads.shape
    refs = [low] + [grads.at[d] for d in range(planes)] + [high]
    for plane, ref in enumerate(refs):
        coarse_rows(tile_of(ref), windows, plane, 0, chans, chans)
    half = weights.shape[1] // 2
    span = cells // 2
    for d in range(planes):
        for start in range(0, cells, span):
            value = None
            for kd in range(3):
                for kh in range(3):
                    begin = start + kh * LANES
                    part = nn(weights[kd * 3 + kh], windows[d + kd, :, begin : begin + span])
                    value = part if value is None else value + part
            own[d, :, start : start + span] = value[:half]
            peer[d, :, start : start + span] = value[half:].astype(BF)


def grad_fine_kernel(own, peer, slope, unpool, grads, first_out, last_out):
    planes = own.shape[0]
    for d in range(planes):
        for j in range(TILES):
            lanes = slice(j * LANES, (j + 1) * LANES)
            block = (own[d, :, lanes] + peer[d, :, lanes].astype(F32)).astype(BF)
            wide = nn(block, unpool[...])
            for side in range(2):
                part = wide[:, side * LANES : (side + 1) * LANES]
                for a in range(2):
                    for row in (side * HH // 2 + 2 * j, side * HH // 2 + 2 * j + 1):
                        cells = slice(row * LANES, (row + 1) * LANES)
                        value = (part * slope[2 * d + a, :, cells].astype(F32)).astype(BF)
                        grads[2 * d + a, :, cells] = value
                        if 2 * d + a == 0:
                            first_out[:, cells] = value
                        if 2 * d + a == 2 * planes - 1:
                            last_out[:, cells] = value


def kernel_grad_fine_kernel(filt, own, low, high, edge, middle, plow, phigh, grads, out, windows, total):
    planes, _, cells = own.shape
    volume_windows(filt, (own, low, high, edge, middle, plow, phigh), windows)
    group = windows.shape[1]
    outs = grads.shape[0] // planes
    seen = set()
    for p in range(planes + 2):
        first, last = max(p - 2, 0), min(p, planes - 1)
        for kh in range(3):
            value = nt(
                windows[p, :, kh * LANES : kh * LANES + cells],
                grads[first * outs : (last + 1) * outs, :],
            )
            for d in range(first, last + 1):
                index = (p - d) * 3 + kh
                rows = slice(index * group, (index + 1) * group)
                part = value[:, (d - first) * outs : (d - first + 1) * outs]
                total[rows, :] = total[rows, :] + part if index in seen else part
                seen.add(index)
    out[...] = total[...].astype(out.dtype)


def backward_fine_kernel(first, count, grads, low, high, weights, own, peer, windows):
    planes, chans, _ = grads.shape

    def put(ref, plane):
        fine_rows(row_of(ref), windows, plane, 0, chans, chans, first, count)

    each(planes, lambda d: put(grads.at[d], d + 1))
    put(low, 0)
    put(high, planes + 1)
    outs = weights.shape[1] // 3
    half = outs // 2
    span = 2 * LANES

    def chunk(j, _):
        totals = [None] * planes
        for p in range(planes + 2):
            value = None
            for kh in range(3):
                lanes = pl.ds(pl.multiple_of((2 * j + kh) * LANES, LANES), span)
                part = nn(weights[kh], windows[p, :, lanes])
                value = part if value is None else value + part
            for kd in range(3):
                d = p - kd
                if 0 <= d < planes:
                    piece = value[kd * outs : (kd + 1) * outs]
                    totals[d] = piece if totals[d] is None else totals[d] + piece
        cells = pl.ds(pl.multiple_of(j * span, span), span)
        for d in range(planes):
            own[d, :, cells] = totals[d][:half]
            peer[d, :, cells] = totals[d][half:].astype(BF)
        return 0

    lax.fori_loop(0, count // 2, chunk, 0, unroll=2)


def to_next(value):
    count = lax.axis_size("depth")
    return lax.ppermute(value, "depth", [(i, i + 1) for i in range(count - 1)])


def to_previous(value):
    count = lax.axis_size("depth")
    return lax.ppermute(value, "depth", [(i + 1, i) for i in range(count - 1)])


def swap(value):
    return lax.ppermute(value, "filt", [(0, 1), (1, 0)])


def halves(value, bit):
    upper = (lax.axis_index("depth") & bit) != 0
    half = value.shape[0] // 2
    return (
        jnp.where(upper, value[half:], value[:half]),
        jnp.where(upper, value[:half], value[half:]),
    )


def across(value, bit):
    count = lax.axis_size("depth")
    return lax.ppermute(value, "depth", [(i, i ^ bit) for i in range(count)])


def plus(a, b):
    return (a.astype(F32) + b.astype(F32)).astype(a.dtype)


def depth_sum(value):
    count = lax.axis_size("depth")
    rows = value.shape[0]
    value = jnp.pad(value, ((0, -rows % 64), (0, 0)))
    near = [bit for bit in (1, 2) if bit < count]
    for bit in near:
        keep, send = halves(value, bit)
        other = yield send, bit
        value = plus(keep, other)
    bit = 4
    while bit < count:
        other = yield value, bit
        value = plus(value, other)
        bit *= 2
    for bit in reversed(near):
        other = yield value, bit
        upper = (lax.axis_index("depth") & bit) != 0
        value = jnp.concatenate(
            [jnp.where(upper, other, value), jnp.where(upper, value, other)], axis=0
        )
    return value[:rows]


class Sum:
    def __init__(self, value):
        self.steps = depth_sum(value)
        self.result = None
        self.take(None)

    def take(self, other):
        try:
            self.pending = self.steps.send(other)
        except StopIteration as stop:
            self.pending, self.result = None, stop.value

    def finish(self):
        while self.pending is not None:
            self.take(across(*self.pending))
        return self.result


def beside(sums, kernel, inputs):
    sums = [one for one in sums if one.pending is not None]
    sends = [one.pending[0] for one in sums]
    inputs, sends = lax.optimization_barrier((list(inputs), sends))
    others = [across(send, one.pending[1]) for send, one in zip(sends, sums)]
    outs, others = lax.optimization_barrier((kernel(*inputs), others))
    for one, other in zip(sums, others):
        one.take(other)
    return outs


def after(value, *others):
    return lax.optimization_barrier((value, *others))[0]


def pool_matrix():
    lane = np.arange(2 * LANES)
    column = np.where(lane < LANES, lane // 2, LANES // 2 + (lane - LANES) // 2)
    return (np.arange(LANES)[None] == column[:, None]) * np.float32(0.125)


def spread_matrix(tall, broad):
    lane = np.arange(4 * tall * broad)
    tile, half, w = lane // LANES, lane % LANES // (2 * broad), lane % (2 * broad)
    row = tile + half * TILES
    cell = row // 2 * broad + w // 2
    return (np.arange(tall * broad)[:, None] == cell[None]) * np.float32(0.125)


def body(volume, w_three, w_four, cotangent):
    own_in, planes, cells = volume.shape
    mid = w_three.shape[1]
    c_mid = w_four.shape[0] // 27
    outs = w_four.shape[1]
    half_planes = planes // 2
    coarse = cells // 4
    filt = lax.axis_index("filt")
    which = filt.astype(jnp.int32).reshape(1)

    own = volume.transpose(1, 0, 2)
    edge = swap(jnp.stack([own[0], own[planes - 1]]))
    middle = swap(own[1 : planes - 1])
    low, high = to_next(own[planes - 1]), to_previous(own[0])
    plow, phigh = to_next(edge[1]), to_previous(edge[0])

    fine = w_three.reshape(3, 3, 3, 2 * own_in, mid)
    fine_forward = fine.transpose(1, 0, 4, 2, 3).reshape(3, 3 * mid, 6 * own_in)
    turned = fine[::-1, ::-1, ::-1].reshape(3, 3, 3, 2, own_in, mid)
    turned = jnp.where(filt == 0, turned, turned[:, :, :, ::-1])
    fine_backward = turned.transpose(1, 0, 3, 4, 2, 5).reshape(3, 6 * own_in, 3 * mid)
    wide = w_four.reshape(3, 3, 3, c_mid, outs)
    wide_forward = wide.transpose(0, 1, 4, 2, 3).reshape(9, outs, 3 * c_mid)
    turned = wide[::-1, ::-1, ::-1].reshape(3, 3, 3, 2, mid, outs)
    turned = jnp.where(filt == 0, turned, turned[:, :, :, ::-1])
    wide_backward = turned.transpose(0, 1, 3, 4, 2, 5).reshape(9, c_mid, 3 * outs)
    pool = jnp.asarray(pool_matrix(), BF)
    unpool = jnp.asarray(pool_matrix().T, BF)
    spread = jnp.asarray(spread_matrix(HH // 4, WW // 4), BF)

    fine_forward, fine_backward, wide_forward, wide_backward, middle = lax.optimization_barrier(
        (fine_forward, fine_backward, wide_forward, wide_backward, middle)
    )

    fine_windows = pltpu.VMEM((planes + 2, 6 * own_in, (HH + 2) * LANES), BF)
    pooled, slope = call(
        forward_fine_kernel,
        [((half_planes, mid, coarse), BF), ((planes, mid, cells), BF)],
        "forward_fine",
        [fine_windows],
        scalars=1,
        inputs=9,
        gflop=17.0,
    )(which, own, low, high, edge, middle, plow, phigh, fine_forward, pool)

    pooled_peer = swap(pooled)
    pool_low = to_next(jnp.stack([pooled[half_planes - 1], pooled_peer[half_planes - 1]]))
    pool_high = to_previous(jnp.stack([pooled[0], pooled_peer[0]]))
    coarse_lanes = (TILES + 2) * LANES
    grad_four, coarse_windows, four_first, four_last = call(
        forward_coarse_kernel,
        [
            ((half_planes, outs, coarse), BF),
            ((half_planes + 2, 3 * c_mid, coarse_lanes), BF),
            ((outs, coarse), BF),
            ((outs, coarse), BF),
        ],
        "forward_coarse",
        scalars=1,
        inputs=7,
        gflop=6.0,
    )(
        which,
        pooled,
        pooled_peer,
        pool_low,
        pool_high,
        wide_forward,
        cotangent.reshape(outs, -1),
        spread,
    )

    four_low, four_high = to_next(four_last), to_previous(four_first)
    (coarse_kernel,) = call(
        kernel_grad_coarse_kernel,
        [((27 * c_mid, outs), BF)],
        "kernel_grad_coarse",
        [pltpu.VMEM((27 * c_mid, outs), F32)],
        inputs=2,
        gflop=6.0,
    )(coarse_windows, grad_four.reshape(half_planes * outs, coarse))
    coarse_sum = Sum(coarse_kernel)
    own_back, peer_back = beside(
        [coarse_sum],
        call(
            backward_coarse_kernel,
            [((half_planes, mid, coarse), F32), ((half_planes, mid, coarse), BF)],
            "backward_coarse",
            [pltpu.VMEM((half_planes + 2, 3 * outs, coarse_lanes), BF)],
            inputs=4,
            gflop=5.0,
        ),
        (grad_four, four_low, four_high, wide_backward),
    )
    (peer_back,) = beside([coarse_sum], lambda value: (swap(value),), (peer_back,))

    grad_three, three_first, three_last = call(
        grad_fine_kernel,
        [((planes, mid, cells), BF), ((mid, cells), BF), ((mid, cells), BF)],
        "grad_fine",
        inputs=4,
        gflop=3.0,
    )(own_back, peer_back, slope, unpool)
    three_low, three_high = to_next(three_last), to_previous(three_first)
    (fine_kernel,) = beside(
        [coarse_sum],
        call(
            kernel_grad_fine_kernel,
            [((54 * own_in, mid), BF)],
            "kernel_grad_fine",
            [fine_windows, pltpu.VMEM((54 * own_in, mid), F32)],
            scalars=1,
            inputs=8,
            gflop=15.0,
        ),
        (which, own, low, high, edge, middle, plow, phigh, grad_three.reshape(planes * mid, cells)),
    )

    fine_sum = Sum(fine_kernel.reshape(27 * own_in, 2 * mid))
    parts = 4
    rows = HH // parts
    owns, peers = [], []
    for part in range(parts):
        mine, theirs = beside(
            [fine_sum, coarse_sum],
            call(
                functools.partial(backward_fine_kernel, part * rows, rows),
                [((planes, own_in, rows * WW), F32), ((planes, own_in, rows * WW), BF)],
                f"backward_fine_{part}",
                [pltpu.VMEM((planes + 2, 3 * mid, (rows + 2) * LANES), BF)],
                inputs=4,
                gflop=6.0,
            ),
            (grad_three, three_low, three_high, fine_backward),
        )
        owns.append(mine)
        peers.append(swap(theirs))
    coarse_sum = coarse_sum.finish()
    fine_sum = fine_sum.finish().reshape(54 * own_in, mid)
    x_grad = jnp.concatenate([a + b.astype(F32) for a, b in zip(owns, peers)], axis=2)
    x_grad = x_grad.transpose(1, 0, 2)

    all_cells = planes * lax.axis_size("depth") * cells
    scale_four = 1.0 / math.sqrt(all_cells / 8.0)
    scale_three = 1.0 / math.sqrt(all_cells * 1.0)
    return (x_grad, fine_sum.astype(F32) * scale_three, coarse_sum.astype(F32) * scale_four)


def solution(mesh):
    return jax.shard_map(
        body,
        mesh=mesh,
        in_specs=(
            P("filt", "depth", None),
            P(None, "filt"),
            P(None, "filt"),
            P("filt", "depth", None),
        ),
        out_specs=(P("filt", "depth", None), P(None, "filt"), P(None, "filt")),
        check_vma=False,
    )
```

```python
import functools
import math

import jax
import jax.numpy as jnp
import numpy as np
from jax import lax
from jax.experimental import pallas as pl
from jax.experimental.pallas import tpu as pltpu
from jax.sharding import PartitionSpec as P

HH = 32
WW = 128
LANES = 128
BF = jnp.bfloat16
F32 = jnp.float32
VMEM_LIMIT = 28 * 2**20
TILES = HH // 4
ROWS = 16
EARLY = HH // 2 + 1


def nn(a, b):
    return jnp.dot(a, b, preferred_element_type=F32)


def nt(a, b):
    return lax.dot_general(a, b, (((1,), (1,)), ((), ())), preferred_element_type=F32)


def call(body, outs, name, scratch=(), scalars=0, inputs=0):
    specs = [pl.BlockSpec(memory_space=pltpu.SMEM)] * scalars
    specs += [pl.BlockSpec(memory_space=pltpu.VMEM)] * inputs
    return pl.pallas_call(
        body,
        out_shape=[jax.ShapeDtypeStruct(shape, dtype) for shape, dtype in outs],
        in_specs=specs,
        out_specs=[pl.BlockSpec(memory_space=pltpu.VMEM)] * len(outs),
        scratch_shapes=list(scratch),
        compiler_params=pltpu.CompilerParams(vmem_limit_bytes=VMEM_LIMIT),
        name=name,
    )


def sigmoid(value):
    return 0.5 * jnp.tanh(0.5 * value) + 0.5


def shifted(block, width):
    lane = lax.broadcasted_iota(jnp.int32, block.shape, 1) % width
    zero = jnp.zeros(block.shape, BF)
    before = jnp.where(lane == 0, zero, pltpu.roll(block, 1, axis=1))
    after = jnp.where(lane == width - 1, zero, pltpu.roll(block, LANES - 1, axis=1))
    return before, after


def fine_rows(source, windows, plane, offset, chans, group, first, lower, upper):

    def row(step):
        block = source(step)
        before, after = shifted(block, WW)
        lanes = pl.ds(pl.multiple_of((step - first + 1) * LANES, LANES), LANES)
        for shift, value in enumerate((before, block, after)):
            windows[plane, pl.ds(pl.multiple_of(shift * group + offset, 32), chans), lanes] = value

    def several(turn, _):
        for k in range(ROWS):
            row(lower + turn * ROWS + k)
        return 0

    zero = jnp.zeros((chans, LANES), BF)
    for shift in range(3):
        rows = pl.ds(pl.multiple_of(shift * group + offset, 32), chans)
        if lower == 0 and first == 0:
            windows[plane, rows, 0:LANES] = zero
        if upper == HH:
            windows[plane, rows, (HH + 1 - first) * LANES : (HH + 2 - first) * LANES] = zero
    if upper - lower >= ROWS:
        lax.fori_loop(0, (upper - lower) // ROWS, several, 0)
    for step in range(upper - (upper - lower) % ROWS, upper):
        row(step)


def row_of(ref, base=0):
    def source(step):
        return ref[:, pl.ds(pl.multiple_of((step - base) * LANES, LANES), LANES)]

    return source


def coarse_rows(source, windows, plane, offset, chans, group):
    half = LANES // 2
    lane = lax.broadcasted_iota(jnp.int32, (chans, LANES), 1)

    def put(shift, tile, value):
        rows = pl.ds(pl.multiple_of(shift * group + offset, 32), chans)
        windows[plane, rows, tile * LANES : (tile + 1) * LANES] = value

    for tile in range(TILES):
        block = source(tile)
        before, after = shifted(block, half)
        for shift, value in enumerate((before, block, after)):
            put(shift, tile + 1, value)
            if tile == 0 or tile == TILES - 1:
                turned = pltpu.roll(value.astype(F32), half, axis=1)
                if tile == TILES - 1:
                    put(shift, 0, jnp.where(lane < half, 0.0, turned).astype(BF))
                else:
                    put(shift, TILES + 1, jnp.where(lane < half, turned, 0.0).astype(BF))


def tile_of(ref):
    def source(tile):
        return ref[:, tile * LANES : (tile + 1) * LANES]

    return source


def each(count, build):
    def step(d, _):
        build(d)
        return 0

    lax.fori_loop(0, count, step, 0)


def volume_windows(filt, refs, windows, first, count):
    own, low, high, peer_low, peer_high, edge, early = refs[:7]
    planes, chans, _ = own.shape
    mine = pl.multiple_of(filt[0] * chans, 32)
    theirs = pl.multiple_of((1 - filt[0]) * chans, 32)
    lower = max(first - 1, 0)
    upper = min(first + count + 1, HH)

    def put(source, plane, offset, start=lower, end=upper):
        fine_rows(source, windows, plane, offset, chans, 2 * chans, first, start, end)

    def inner(d):
        if lower < EARLY:
            put(row_of(early.at[d]), d + 2, theirs, lower, min(upper, EARLY))
        if upper > EARLY:
            put(row_of(refs[7].at[d], EARLY), d + 2, theirs, max(lower, EARLY), upper)

    each(planes, lambda d: put(row_of(own.at[d]), d + 1, mine))
    each(planes - 2, inner)
    each(2, lambda d: put(row_of(edge.at[d]), 1 + d * (planes - 1), theirs))
    put(row_of(low), 0, mine)
    put(row_of(high), planes + 1, mine)
    put(row_of(peer_low), 0, theirs)
    put(row_of(peer_high), planes + 1, theirs)


def forward_fine_kernel(first, count, volumes, filt, *refs):
    weights, pool = refs[volumes : volumes + 2]
    pooled, slope, windows = refs[-3:]
    before = refs[volumes + 2] if first > 0 else None
    planes = refs[0].shape[0]
    volume_windows(filt, refs[:volumes], windows, first, count)
    outs = weights.shape[1] // 3
    span = 2 * LANES
    side = slice(0, LANES) if first == 0 else slice(LANES, 2 * LANES)

    def chunk(j, _):
        totals = [None] * planes
        for p in range(planes + 2):
            value = None
            for kh in range(3):
                lanes = pl.ds(pl.multiple_of((2 * j + kh) * LANES, LANES), span)
                part = nn(weights[kh], windows[p, :, lanes])
                value = part if value is None else value + part
            for kd in range(3):
                d = p - kd
                if 0 <= d < planes:
                    piece = value[kd * outs : (kd + 1) * outs]
                    totals[d] = piece if totals[d] is None else totals[d] + piece
        acts = []
        for d in range(planes):
            pre = totals[d]
            sigma = sigmoid(pre)
            act = pre * sigma
            slope[d, :, pl.ds(pl.multiple_of(j * span, span), span)] = (
                sigma + act * (1.0 - sigma)
            ).astype(BF)
            acts.append(act[:, :LANES] + act[:, LANES:])
        tile = pl.ds(pl.multiple_of(j * LANES, LANES), LANES)
        for d in range(planes // 2):
            both = acts[2 * d] + acts[2 * d + 1]
            coarse = both.astype(BF)
            rest = (both - coarse.astype(F32)).astype(BF)
            mean = nn(coarse, pool[side, :]) + nn(rest, pool[side, :])
            if before is not None:
                mean = mean + before[d, :, tile].astype(F32)
            pooled[d, :, tile] = mean.astype(BF)
        return 0

    lax.fori_loop(0, count // 2, chunk, 0, unroll=2)


def forward_coarse_kernel(filt, own, peer, low, high, weights, cot, spread, grads, windows, first_out, last_out):
    planes, chans, cells = own.shape
    mine = pl.multiple_of(filt[0] * chans, 32)
    theirs = pl.multiple_of((1 - filt[0]) * chans, 32)
    sides = ((mine, low.at[0], own, high.at[0]), (theirs, low.at[1], peer, high.at[1]))
    for offset, below, middle, above in sides:
        refs = [below] + [middle.at[d] for d in range(planes)] + [above]
        for plane, ref in enumerate(refs):
            coarse_rows(tile_of(ref), windows, plane, offset, chans, 2 * chans)
    upper = nn(cot[...], spread[...])
    span = cells // 2
    for d in range(planes):
        for start in range(0, cells, span):
            pre = None
            for kd in range(3):
                for kh in range(3):
                    begin = start + kh * LANES
                    part = nn(weights[kd * 3 + kh], windows[d + kd, :, begin : begin + span])
                    pre = part if pre is None else pre + part
            sigma = sigmoid(pre)
            slope = sigma * (1.0 + pre * (1.0 - sigma))
            value = (upper[:, start : start + span] * slope).astype(BF)
            grads[d, :, start : start + span] = value
            if d == 0:
                first_out[:, start : start + span] = value
            if d == planes - 1:
                last_out[:, start : start + span] = value


def kernel_grad_coarse_kernel(windows, grads, out, total):
    deep, group, _ = windows.shape
    planes = deep - 2
    outs = grads.shape[0] // planes
    cells = grads.shape[1]
    seen = set()
    for p in range(deep):
        first, last = max(p - 2, 0), min(p, planes - 1)
        for kh in range(3):
            value = nt(
                windows[p, :, kh * LANES : kh * LANES + cells],
                grads[first * outs : (last + 1) * outs, :],
            )
            for d in range(first, last + 1):
                index = (p - d) * 3 + kh
                rows = slice(index * group, (index + 1) * group)
                part = value[:, (d - first) * outs : (d - first + 1) * outs]
                total[rows, :] = total[rows, :] + part if index in seen else part
                seen.add(index)
    out[...] = total[...].astype(out.dtype)


def pick(filt, value):
    half = value.shape[0] // 2
    first = filt[0] == 0
    return (
        jnp.where(first, value[:half], value[half:]),
        jnp.where(first, value[half:], value[:half]),
    )


def backward_coarse_kernel(filt, grads, low, high, weights, own, peer, windows):
    planes, chans, cells = grads.shape
    refs = [low] + [grads.at[d] for d in range(planes)] + [high]
    for plane, ref in enumerate(refs):
        coarse_rows(tile_of(ref), windows, plane, 0, chans, chans)
    rows = weights.shape[0] // 27
    span = cells // 2
    for d in range(planes):
        for start in range(0, cells, span):
            value = None
            for kd in range(3):
                for kh in range(3):
                    base = ((2 - kd) * 9 + (2 - kh) * 3) * rows
                    taps = jnp.concatenate(
                        [weights[base + k * rows : base + (k + 1) * rows, :] for k in (2, 1, 0)],
                        axis=1,
                    )
                    begin = start + kh * LANES
                    part = nn(taps, windows[d + kd, :, begin : begin + span])
                    value = part if value is None else value + part
            mine, theirs = pick(filt, value)
            own[d, :, start : start + span] = mine
            peer[d, :, start : start + span] = theirs.astype(BF)


def weights_kernel(fine, wide, fine_forward, fine_backward, wide_forward):
    chans = fine.shape[0] // 27
    outs = fine.shape[1]
    for kd in range(3):
        for kh in range(3):
            base = (kd * 3 + kh) * 3 * chans
            block = fine[base : base + 3 * chans, :].astype(F32).T
            fine_forward[kh, kd * outs : (kd + 1) * outs, :] = block.astype(BF)
            base = ((2 - kd) * 9 + (2 - kh) * 3) * chans
            fine_backward[kh, kd * chans : (kd + 1) * chans, :] = jnp.concatenate(
                [fine[base + k * chans : base + (k + 1) * chans, :] for k in (2, 1, 0)], axis=1
            )
    group = wide.shape[0] // 9
    for k in range(9):
        block = wide[k * group : (k + 1) * group, :].astype(F32).T
        wide_forward[k] = block.astype(BF)


def grad_fine_kernel(own, peer, upper, lower, unpool, grads, first_out, last_out):
    planes = own.shape[0]
    for d in range(planes):
        for j in range(TILES):
            lanes = slice(j * LANES, (j + 1) * LANES)
            block = (own[d, :, lanes] + peer[d, :, lanes].astype(F32)).astype(BF)
            wide = nn(block, unpool[...])
            for side in range(2):
                part = wide[:, side * LANES : (side + 1) * LANES]
                for a in range(2):
                    for row in (side * HH // 2 + 2 * j, side * HH // 2 + 2 * j + 1):
                        cells = slice(row * LANES, (row + 1) * LANES)
                        slope = lower if side else upper
                        begin = (row - side * HH // 2) * LANES
                        factor = slope[2 * d + a, :, begin : begin + LANES].astype(F32)
                        value = (part * factor).astype(BF)
                        grads[2 * d + a, :, cells] = value
                        if 2 * d + a == 0:
                            first_out[:, cells] = value
                        if 2 * d + a == 2 * planes - 1:
                            last_out[:, cells] = value


def kernel_grad_fine_kernel(filt, *refs):
    grads, out, windows, total = refs[-4:]
    planes, _, cells = refs[0].shape
    volume_windows(filt, refs[:-4], windows, 0, HH)
    group = windows.shape[1]
    outs = grads.shape[0] // planes
    seen = set()
    for p in range(planes + 2):
        first, last = max(p - 2, 0), min(p, planes - 1)
        for kh in range(3):
            value = nt(
                windows[p, :, kh * LANES : kh * LANES + cells],
                grads[first * outs : (last + 1) * outs, :],
            )
            for d in range(first, last + 1):
                index = (p - d) * 3 + kh
                rows = slice(index * group, (index + 1) * group)
                part = value[:, (d - first) * outs : (d - first + 1) * outs]
                total[rows, :] = total[rows, :] + part if index in seen else part
                seen.add(index)
    out[...] = total[...].astype(out.dtype)


def backward_fine_kernel(first, count, filt, grads, low, high, weights, own, peer, windows):
    planes, chans, _ = grads.shape

    def put(ref, plane):
        lower, upper = max(first - 1, 0), min(first + count + 1, HH)
        fine_rows(row_of(ref), windows, plane, 0, chans, chans, first, lower, upper)

    each(planes, lambda d: put(grads.at[d], d + 1))
    put(low, 0)
    put(high, planes + 1)
    outs = weights.shape[1] // 3
    span = 2 * LANES

    def chunk(j, _):
        totals = [None] * planes
        for p in range(planes + 2):
            value = None
            for kh in range(3):
                lanes = pl.ds(pl.multiple_of((2 * j + kh) * LANES, LANES), span)
                part = nn(weights[kh], windows[p, :, lanes])
                value = part if value is None else value + part
            for kd in range(3):
                d = p - kd
                if 0 <= d < planes:
                    piece = value[kd * outs : (kd + 1) * outs]
                    totals[d] = piece if totals[d] is None else totals[d] + piece
        cells = pl.ds(pl.multiple_of(j * span, span), span)
        for d in range(planes):
            mine, theirs = pick(filt, totals[d])
            own[d, :, cells] = mine
            peer[d, :, cells] = theirs.astype(BF)
        return 0

    lax.fori_loop(0, count // 2, chunk, 0, unroll=2)


def to_next(value):
    count = lax.axis_size("depth")
    return lax.ppermute(value, "depth", [(i, i + 1) for i in range(count - 1)])


def to_previous(value):
    count = lax.axis_size("depth")
    return lax.ppermute(value, "depth", [(i + 1, i) for i in range(count - 1)])


def swap(value):
    return lax.ppermute(value, "filt", [(0, 1), (1, 0)])


def halves(value, bit):
    upper = (lax.axis_index("depth") & bit) != 0
    half = value.shape[0] // 2
    return (
        jnp.where(upper, value[half:], value[:half]),
        jnp.where(upper, value[:half], value[half:]),
    )


def across(value, bit):
    count = lax.axis_size("depth")
    return lax.ppermute(value, "depth", [(i, i ^ bit) for i in range(count)])


def plus(a, b):
    return (a.astype(F32) + b.astype(F32)).astype(a.dtype)


def depth_sum(value):
    count = lax.axis_size("depth")
    rows = value.shape[0]
    value = jnp.pad(value, ((0, -rows % 64), (0, 0)))
    near = [bit for bit in (1, 2) if bit < count]
    for bit in near:
        keep, send = halves(value, bit)
        other = yield send, bit
        value = plus(keep, other)
    bit = 4
    while bit < count:
        other = yield value, bit
        value = plus(value, other)
        bit *= 2
    for bit in reversed(near):
        other = yield value, bit
        upper = (lax.axis_index("depth") & bit) != 0
        value = jnp.concatenate(
            [jnp.where(upper, other, value), jnp.where(upper, value, other)], axis=0
        )
    return value[:rows]


class Sum:
    def __init__(self, value):
        self.steps = depth_sum(value)
        self.result = None
        self.take(None)

    def take(self, other):
        try:
            self.pending = self.steps.send(other)
        except StopIteration as stop:
            self.pending, self.result = None, stop.value

    def finish(self):
        while self.pending is not None:
            self.take(across(*self.pending))
        return self.result


def beside(sums, kernel, inputs, swapped=()):
    sums = [one for one in sums if one.pending is not None]
    sends = [one.pending[0] for one in sums]
    inputs, sends, swapped = lax.optimization_barrier((list(inputs), sends, list(swapped)))
    others = [across(send, one.pending[1]) for send, one in zip(sends, sums)]
    swapped = [swap(value) for value in swapped]
    outs, others, swapped = lax.optimization_barrier((kernel(*inputs), others, swapped))
    for one, other in zip(sums, others):
        one.take(other)
    return outs, swapped


def after(value, *others):
    return lax.optimization_barrier((value, *others))[0]


def pool_matrix():
    lane = np.arange(2 * LANES)
    column = np.where(lane < LANES, lane // 2, LANES // 2 + (lane - LANES) // 2)
    return (np.arange(LANES)[None] == column[:, None]) * np.float32(0.125)


def spread_matrix(tall, broad):
    lane = np.arange(4 * tall * broad)
    tile, half, w = lane // LANES, lane % LANES // (2 * broad), lane % (2 * broad)
    row = tile + half * TILES
    cell = row // 2 * broad + w // 2
    return (np.arange(tall * broad)[:, None] == cell[None]) * np.float32(0.125)


def body(volume, w_three, w_four, cotangent):
    own_in, planes, cells = volume.shape
    mid = w_three.shape[1]
    c_mid = w_four.shape[0] // 27
    outs = w_four.shape[1]
    half_planes = planes // 2
    coarse = cells // 4
    filt = lax.axis_index("filt")
    which = filt.astype(jnp.int32).reshape(1)

    own = volume.transpose(1, 0, 2)
    edge = swap(jnp.stack([own[0], own[planes - 1]]))
    early = swap(own[1 : planes - 1, :, : EARLY * WW])
    low, high = to_next(own[planes - 1]), to_previous(own[0])
    late, edge = lax.optimization_barrier((own[1 : planes - 1, :, EARLY * WW :], edge))
    late = swap(late)
    plow, phigh = to_next(edge[1]), to_previous(edge[0])
    volumes = (own, low, high, plow, phigh, edge, early, late)

    fine_forward, fine_backward, wide_forward = call(
        weights_kernel,
        [
            ((3, 3 * mid, 6 * own_in), BF),
            ((3, 6 * own_in, 3 * mid), BF),
            ((9, outs, 3 * c_mid), BF),
        ],
        "weights",
        inputs=2,
    )(w_three, w_four)
    pool = jnp.asarray(pool_matrix(), BF)
    unpool = jnp.asarray(pool_matrix().T, BF)
    spread = jnp.asarray(spread_matrix(HH // 4, WW // 4), BF)

    half = HH // 2
    part_outs = [((half_planes, mid, coarse), BF), ((planes, mid, cells // 2), BF)]
    part_windows = pltpu.VMEM((planes + 2, 6 * own_in, (half + 2) * LANES), BF)
    fine_windows = pltpu.VMEM((planes + 2, 6 * own_in, (HH + 2) * LANES), BF)
    pooled, slope_upper = call(
        functools.partial(forward_fine_kernel, 0, half, 7),
        part_outs,
        "forward_fine_upper",
        [part_windows],
        scalars=1,
        inputs=9,
    )(which, *volumes[:7], fine_forward, pool)
    pooled, slope_lower = call(
        functools.partial(forward_fine_kernel, half, half, 8),
        part_outs,
        "forward_fine_lower",
        [part_windows],
        scalars=1,
        inputs=11,
    )(which, *volumes, fine_forward, pool, pooled)

    pooled_peer = swap(pooled)
    pool_low = to_next(jnp.stack([pooled[half_planes - 1], pooled_peer[half_planes - 1]]))
    pool_high = to_previous(jnp.stack([pooled[0], pooled_peer[0]]))
    coarse_lanes = (TILES + 2) * LANES
    grad_four, coarse_windows, four_first, four_last = call(
        forward_coarse_kernel,
        [
            ((half_planes, outs, coarse), BF),
            ((half_planes + 2, 3 * c_mid, coarse_lanes), BF),
            ((outs, coarse), BF),
            ((outs, coarse), BF),
        ],
        "forward_coarse",
        scalars=1,
        inputs=7,
    )(
        which,
        pooled,
        pooled_peer,
        pool_low,
        pool_high,
        wide_forward,
        cotangent.reshape(outs, -1),
        spread,
    )

    four_low, four_high = to_next(four_last), to_previous(four_first)
    (coarse_kernel,) = call(
        kernel_grad_coarse_kernel,
        [((27 * c_mid, outs), BF)],
        "kernel_grad_coarse",
        [pltpu.VMEM((27 * c_mid, outs), F32)],
        inputs=2,
    )(coarse_windows, grad_four.reshape(half_planes * outs, coarse))
    coarse_sum = Sum(coarse_kernel)
    (own_back, peer_back), _ = beside(
        [coarse_sum],
        call(
            backward_coarse_kernel,
            [((half_planes, mid, coarse), F32), ((half_planes, mid, coarse), BF)],
            "backward_coarse",
            [pltpu.VMEM((half_planes + 2, 3 * outs, coarse_lanes), BF)],
            scalars=1,
            inputs=4,
        ),
        (which, grad_four, four_low, four_high, w_four),
    )
    _, (peer_back,) = beside([coarse_sum], lambda: (), (), [peer_back])

    grad_three, three_first, three_last = call(
        grad_fine_kernel,
        [((planes, mid, cells), BF), ((mid, cells), BF), ((mid, cells), BF)],
        "grad_fine",
        inputs=5,
    )(own_back, peer_back, slope_upper, slope_lower, unpool)
    three_low, three_high = to_next(three_last), to_previous(three_first)
    (fine_kernel,), _ = beside(
        [coarse_sum],
        call(
            kernel_grad_fine_kernel,
            [((54 * own_in, mid), BF)],
            "kernel_grad_fine",
            [fine_windows, pltpu.VMEM((54 * own_in, mid), F32)],
            scalars=1,
            inputs=9,
        ),
        (which, *volumes, grad_three.reshape(planes * mid, cells)),
    )

    fine_sum = Sum(fine_kernel.reshape(27 * own_in, 2 * mid))
    parts = 4
    rows = HH // parts
    owns, peers, theirs = [], [], []
    for part in range(parts):
        (mine, *theirs), came = beside(
            [fine_sum, coarse_sum],
            call(
                functools.partial(backward_fine_kernel, part * rows, rows),
                [((planes, own_in, rows * WW), F32), ((planes, own_in, rows * WW), BF)],
                f"backward_fine_{part}",
                [pltpu.VMEM((planes + 2, 3 * mid, (rows + 2) * LANES), BF)],
                scalars=1,
                inputs=4,
            ),
            (which, grad_three, three_low, three_high, fine_backward),
            theirs,
        )
        owns.append(mine)
        peers += came
    _, came = beside([fine_sum, coarse_sum], lambda: (), (), theirs)
    peers += came
    coarse_sum = coarse_sum.finish()
    fine_sum = fine_sum.finish().reshape(54 * own_in, mid)
    x_grad = jnp.concatenate([a + b.astype(F32) for a, b in zip(owns, peers)], axis=2)
    x_grad = x_grad.transpose(1, 0, 2)

    all_cells = planes * lax.axis_size("depth") * cells
    scale_four = 1.0 / math.sqrt(all_cells / 8.0)
    scale_three = 1.0 / math.sqrt(all_cells * 1.0)
    return (x_grad, fine_sum.astype(F32) * scale_three, coarse_sum.astype(F32) * scale_four)


def solution(mesh):
    return jax.shard_map(
        body,
        mesh=mesh,
        in_specs=(
            P("filt", "depth", None),
            P(None, "filt"),
            P(None, "filt"),
            P("filt", "depth", None),
        ),
        out_specs=(P("filt", "depth", None), P(None, "filt"), P(None, "filt")),
        check_vma=False,
    )
```

```python
import functools
import math

import jax
import jax.numpy as jnp
import numpy as np
from jax import lax
from jax.experimental import pallas as pl
from jax.experimental.pallas import tpu as pltpu
from jax.sharding import PartitionSpec as P

HH = 32
WW = 128
LANES = 128
BF = jnp.bfloat16
F32 = jnp.float32
VMEM_LIMIT = 24 * 2**20
TILES = HH // 4
ROWS = 16


def nn(a, b):
    return jnp.dot(a, b, preferred_element_type=F32)


def nt(a, b):
    return lax.dot_general(a, b, (((1,), (1,)), ((), ())), preferred_element_type=F32)


def call(body, outs, name, scratch=(), scalars=0, inputs=0):
    specs = [pl.BlockSpec(memory_space=pltpu.SMEM)] * scalars
    specs += [pl.BlockSpec(memory_space=pltpu.VMEM)] * inputs
    return pl.pallas_call(
        body,
        out_shape=[jax.ShapeDtypeStruct(shape, dtype) for shape, dtype in outs],
        in_specs=specs,
        out_specs=[pl.BlockSpec(memory_space=pltpu.VMEM)] * len(outs),
        scratch_shapes=list(scratch),
        compiler_params=pltpu.CompilerParams(vmem_limit_bytes=VMEM_LIMIT),
        name=name,
    )


def sigmoid(value):
    return 0.5 * jnp.tanh(0.5 * value) + 0.5


def shifted(block, width):
    lane = lax.broadcasted_iota(jnp.int32, block.shape, 1) % width
    zero = jnp.zeros(block.shape, BF)
    before = jnp.where(lane == 0, zero, pltpu.roll(block, 1, axis=1))
    after = jnp.where(lane == width - 1, zero, pltpu.roll(block, LANES - 1, axis=1))
    return before, after


def fine_rows(source, windows, plane, offset, chans, group, first, lower, upper):

    def row(step):
        block = source(step)
        before, after = shifted(block, WW)
        lanes = pl.ds(pl.multiple_of((step - first + 1) * LANES, LANES), LANES)
        for shift, value in enumerate((before, block, after)):
            windows[plane, pl.ds(pl.multiple_of(shift * group + offset, 32), chans), lanes] = value

    def several(turn, _):
        for k in range(ROWS):
            row(lower + turn * ROWS + k)
        return 0

    zero = jnp.zeros((chans, LANES), BF)
    for shift in range(3):
        rows = pl.ds(pl.multiple_of(shift * group + offset, 32), chans)
        if lower == 0 and first == 0:
            windows[plane, rows, 0:LANES] = zero
        if upper == HH:
            windows[plane, rows, (HH + 1 - first) * LANES : (HH + 2 - first) * LANES] = zero
    if upper - lower >= ROWS:
        lax.fori_loop(0, (upper - lower) // ROWS, several, 0)
    for step in range(upper - (upper - lower) % ROWS, upper):
        row(step)


def row_of(ref, base=0):
    def source(step):
        return ref[:, pl.ds(pl.multiple_of((step - base) * LANES, LANES), LANES)]

    return source


def coarse_rows(source, windows, plane, offset, chans, group):
    half = LANES // 2
    lane = lax.broadcasted_iota(jnp.int32, (chans, LANES), 1)

    def put(shift, tile, value):
        rows = pl.ds(pl.multiple_of(shift * group + offset, 32), chans)
        windows[plane, rows, tile * LANES : (tile + 1) * LANES] = value

    for tile in range(TILES):
        block = source(tile)
        before, after = shifted(block, half)
        for shift, value in enumerate((before, block, after)):
            put(shift, tile + 1, value)
            if tile == 0 or tile == TILES - 1:
                turned = pltpu.roll(value.astype(F32), half, axis=1)
                if tile == TILES - 1:
                    put(shift, 0, jnp.where(lane < half, 0.0, turned).astype(BF))
                else:
                    put(shift, TILES + 1, jnp.where(lane < half, turned, 0.0).astype(BF))


def tile_of(ref):
    def source(tile):
        return ref[:, tile * LANES : (tile + 1) * LANES]

    return source


def each(count, build):
    def step(d, _):
        build(d)
        return 0

    lax.fori_loop(0, count, step, 0)


def volume_windows(filt, refs, windows, first, last):
    own, low, high, peer_low, peer_high, edge, middle = refs
    planes, chans, _ = own.shape
    mine = pl.multiple_of(filt[0] * chans, 32)
    theirs = pl.multiple_of((1 - filt[0]) * chans, 32)

    def put(ref, plane, offset):
        fine_rows(row_of(ref), windows, plane - first, offset, chans, 2 * chans, 0, 0, HH)

    lower, upper = max(first, 1), min(last, planes + 1)
    each(upper - lower, lambda d: put(own.at[d + lower - 1], d + lower, mine))
    lower, upper = max(first, 2), min(last, planes)
    each(upper - lower, lambda d: put(middle.at[d + lower - 2], d + lower, theirs))
    if first == 0 and last == planes + 2:
        each(2, lambda d: put(edge.at[d], 1 + d * (planes - 1), theirs))
    elif first == 0:
        put(edge.at[0], 1, theirs)
    else:
        put(edge.at[1], planes, theirs)
    if first == 0:
        put(low, 0, mine)
        put(peer_low, 0, theirs)
    if last == planes + 2:
        put(high, planes + 1, mine)
        put(peer_high, planes + 1, theirs)


def forward_fine_kernel(filt, *refs):
    weights, pool, pooled, slope, windows = refs[-5:]
    planes = refs[0].shape[0]
    volume_windows(filt, refs[:-5], windows, 0, planes + 2)
    outs = weights.shape[1] // 3
    span = 2 * LANES

    def chunk(j, _):
        acts = [[None, None] for _ in range(planes)]
        for side in range(2):
            top = side * (HH // 2) + j * 2
            totals = [None] * planes
            for p in range(planes + 2):
                value = None
                for kh in range(3):
                    lanes = pl.ds(pl.multiple_of((top + kh) * LANES, LANES), span)
                    part = nn(weights[kh], windows[p, :, lanes])
                    value = part if value is None else value + part
                for kd in range(3):
                    d = p - kd
                    if 0 <= d < planes:
                        piece = value[kd * outs : (kd + 1) * outs]
                        totals[d] = piece if totals[d] is None else totals[d] + piece
            for d in range(planes):
                pre = totals[d]
                sigma = sigmoid(pre)
                act = pre * sigma
                slope[d, :, pl.ds(pl.multiple_of(top * LANES, LANES), span)] = (
                    sigma + act * (1.0 - sigma)
                ).astype(BF)
                acts[d][side] = act[:, :LANES] + act[:, LANES:]
        for d in range(0, planes, 2):
            both = jnp.concatenate(
                [acts[d][0] + acts[d + 1][0], acts[d][1] + acts[d + 1][1]], axis=1
            )
            coarse = both.astype(BF)
            rest = (both - coarse.astype(F32)).astype(BF)
            mean = nn(coarse, pool[...]) + nn(rest, pool[...])
            pooled[d // 2, :, pl.ds(pl.multiple_of(j * LANES, LANES), LANES)] = mean.astype(BF)
        return 0

    lax.fori_loop(0, TILES, chunk, 0, unroll=2)


def forward_coarse_kernel(filt, own, peer, low, high, weights, cot, spread, grads, windows, first_out, last_out):
    planes, chans, cells = own.shape
    mine = pl.multiple_of(filt[0] * chans, 32)
    theirs = pl.multiple_of((1 - filt[0]) * chans, 32)
    sides = ((mine, low.at[0], own, high.at[0]), (theirs, low.at[1], peer, high.at[1]))
    for offset, below, middle, above in sides:
        refs = [below] + [middle.at[d] for d in range(planes)] + [above]
        for plane, ref in enumerate(refs):
            coarse_rows(tile_of(ref), windows, plane, offset, chans, 2 * chans)
    upper = nn(cot[...], spread[...])
    span = cells // 2
    for d in range(planes):
        for start in range(0, cells, span):
            pre = None
            for kd in range(3):
                for kh in range(3):
                    begin = start + kh * LANES
                    part = nn(weights[kd * 3 + kh], windows[d + kd, :, begin : begin + span])
                    pre = part if pre is None else pre + part
            sigma = sigmoid(pre)
            slope = sigma * (1.0 + pre * (1.0 - sigma))
            value = (upper[:, start : start + span] * slope).astype(BF)
            grads[d, :, start : start + span] = value
            if d == 0:
                first_out[:, start : start + span] = value
            if d == planes - 1:
                last_out[:, start : start + span] = value


def kernel_grad_coarse_kernel(windows, grads, out, total):
    deep, group, _ = windows.shape
    planes = deep - 2
    outs = grads.shape[0] // planes
    cells = grads.shape[1]
    seen = set()
    for p in range(deep):
        first, last = max(p - 2, 0), min(p, planes - 1)
        for kh in range(3):
            value = nt(
                windows[p, :, kh * LANES : kh * LANES + cells],
                grads[first * outs : (last + 1) * outs, :],
            )
            for d in range(first, last + 1):
                index = (p - d) * 3 + kh
                rows = slice(index * group, (index + 1) * group)
                part = value[:, (d - first) * outs : (d - first + 1) * outs]
                total[rows, :] = total[rows, :] + part if index in seen else part
                seen.add(index)
    out[...] = total[...].astype(out.dtype)


def pick(filt, value):
    half = value.shape[0] // 2
    first = filt[0] == 0
    return (
        jnp.where(first, value[:half], value[half:]),
        jnp.where(first, value[half:], value[:half]),
    )


def backward_coarse_kernel(filt, grads, low, high, weights, own, peer, windows):
    planes, chans, cells = grads.shape
    refs = [low] + [grads.at[d] for d in range(planes)] + [high]
    for plane, ref in enumerate(refs):
        coarse_rows(tile_of(ref), windows, plane, 0, chans, chans)
    rows = weights.shape[0] // 27
    span = cells // 2
    for d in range(planes):
        for start in range(0, cells, span):
            value = None
            for kd in range(3):
                for kh in range(3):
                    base = ((2 - kd) * 9 + (2 - kh) * 3) * rows
                    taps = jnp.concatenate(
                        [weights[base + k * rows : base + (k + 1) * rows, :] for k in (2, 1, 0)],
                        axis=1,
                    )
                    begin = start + kh * LANES
                    part = nn(taps, windows[d + kd, :, begin : begin + span])
                    value = part if value is None else value + part
            mine, theirs = pick(filt, value)
            own[d, :, start : start + span] = mine
            peer[d, :, start : start + span] = theirs.astype(BF)


def weights_kernel(fine, wide, fine_forward, fine_backward, wide_forward):
    chans = fine.shape[0] // 27
    outs = fine.shape[1]
    for kd in range(3):
        for kh in range(3):
            base = (kd * 3 + kh) * 3 * chans
            block = fine[base : base + 3 * chans, :].astype(F32).T
            fine_forward[kh, kd * outs : (kd + 1) * outs, :] = block.astype(BF)
            base = ((2 - kd) * 9 + (2 - kh) * 3) * chans
            fine_backward[kh, kd * chans : (kd + 1) * chans, :] = jnp.concatenate(
                [fine[base + k * chans : base + (k + 1) * chans, :] for k in (2, 1, 0)], axis=1
            )
    group = wide.shape[0] // 9
    for k in range(9):
        block = wide[k * group : (k + 1) * group, :].astype(F32).T
        wide_forward[k] = block.astype(BF)


def grad_fine_kernel(own, peer, slope, unpool, grads, first_out, last_out):
    planes = own.shape[0]
    for d in range(planes):
        for j in range(TILES):
            lanes = slice(j * LANES, (j + 1) * LANES)
            block = (own[d, :, lanes] + peer[d, :, lanes].astype(F32)).astype(BF)
            wide = nn(block, unpool[...])
            for side in range(2):
                part = wide[:, side * LANES : (side + 1) * LANES]
                for a in range(2):
                    for row in (side * HH // 2 + 2 * j, side * HH // 2 + 2 * j + 1):
                        cells = slice(row * LANES, (row + 1) * LANES)
                        factor = slope[2 * d + a, :, cells].astype(F32)
                        value = (part * factor).astype(BF)
                        grads[2 * d + a, :, cells] = value
                        if 2 * d + a == 0:
                            first_out[:, cells] = value
                        if 2 * d + a == 2 * planes - 1:
                            last_out[:, cells] = value


def kernel_grad_fine_kernel(start, end, filt, *refs):
    grads = refs[7]
    out, windows = refs[-2:]
    before = refs[8] if start > 0 else None
    planes, _, cells = refs[0].shape
    volume_windows(filt, refs[:7], windows, start, end)
    group = windows.shape[1]
    outs = grads.shape[0] // planes
    seen = set()
    for p in range(start, end):
        first, last = max(p - 2, 0), min(p, planes - 1)
        for kh in range(3):
            value = nt(
                windows[p - start, :, kh * LANES : kh * LANES + cells],
                grads[first * outs : (last + 1) * outs, :],
            )
            for d in range(first, last + 1):
                index = (p - d) * 3 + kh
                rows = slice(index * group, (index + 1) * group)
                part = value[:, (d - first) * outs : (d - first + 1) * outs]
                if index in seen:
                    part = out[rows, :] + part
                elif before is not None:
                    part = before[rows, :] + part
                out[rows, :] = part
                seen.add(index)


def backward_fine_kernel(first, count, filt, grads, low, high, weights, own, peer, windows):
    planes, chans, _ = grads.shape

    def put(ref, plane):
        lower, upper = max(first - 1, 0), min(first + count + 1, HH)
        fine_rows(row_of(ref), windows, plane, 0, chans, chans, first, lower, upper)

    each(planes, lambda d: put(grads.at[d], d + 1))
    put(low, 0)
    put(high, planes + 1)
    outs = weights.shape[1] // 3
    span = 2 * LANES

    def chunk(j, _):
        totals = [None] * planes
        for p in range(planes + 2):
            value = None
            for kh in range(3):
                lanes = pl.ds(pl.multiple_of((2 * j + kh) * LANES, LANES), span)
                part = nn(weights[kh], windows[p, :, lanes])
                value = part if value is None else value + part
            for kd in range(3):
                d = p - kd
                if 0 <= d < planes:
                    piece = value[kd * outs : (kd + 1) * outs]
                    totals[d] = piece if totals[d] is None else totals[d] + piece
        cells = pl.ds(pl.multiple_of(j * span, span), span)
        for d in range(planes):
            mine, theirs = pick(filt, totals[d])
            own[d, :, cells] = mine
            peer[d, :, cells] = theirs.astype(BF)
        return 0

    lax.fori_loop(0, count // 2, chunk, 0, unroll=2)


def to_next(value):
    count = lax.axis_size("depth")
    return lax.ppermute(value, "depth", [(i, i + 1) for i in range(count - 1)])


def to_previous(value):
    count = lax.axis_size("depth")
    return lax.ppermute(value, "depth", [(i + 1, i) for i in range(count - 1)])


def swap(value):
    return lax.ppermute(value, "filt", [(0, 1), (1, 0)])


def halves(value, bit):
    upper = (lax.axis_index("depth") & bit) != 0
    half = value.shape[0] // 2
    return (
        jnp.where(upper, value[half:], value[:half]),
        jnp.where(upper, value[:half], value[half:]),
    )


def across(value, bit):
    count = lax.axis_size("depth")
    return lax.ppermute(value, "depth", [(i, i ^ bit) for i in range(count)])


def plus(a, b):
    return (a.astype(F32) + b.astype(F32)).astype(a.dtype)


def depth_sum(value):
    count = lax.axis_size("depth")
    rows = value.shape[0]
    value = jnp.pad(value, ((0, -rows % 64), (0, 0)))
    near = [bit for bit in (1, 2) if bit < count]
    for bit in near:
        keep, send = halves(value, bit)
        other = yield send, bit
        value = plus(keep, other)
    bit = 4
    while bit < count:
        other = yield value, bit
        value = plus(value, other)
        bit *= 2
    for bit in reversed(near):
        other = yield value, bit
        upper = (lax.axis_index("depth") & bit) != 0
        value = jnp.concatenate(
            [jnp.where(upper, other, value), jnp.where(upper, value, other)], axis=0
        )
    return value[:rows]


class Sum:
    def __init__(self, value):
        self.steps = depth_sum(value)
        self.result = None
        self.take(None)

    def take(self, other):
        try:
            self.pending = self.steps.send(other)
        except StopIteration as stop:
            self.pending, self.result = None, stop.value

    def finish(self):
        while self.pending is not None:
            self.take(across(*self.pending))
        return self.result


def beside(sums, kernel, inputs, swapped=()):
    sums = [one for one in sums if one.pending is not None]
    sends = [one.pending[0] for one in sums]
    inputs, sends, swapped = lax.optimization_barrier((list(inputs), sends, list(swapped)))
    others = [across(send, one.pending[1]) for send, one in zip(sends, sums)]
    swapped = [swap(value) for value in swapped]
    outs, others, swapped = lax.optimization_barrier((kernel(*inputs), others, swapped))
    for one, other in zip(sums, others):
        one.take(other)
    return outs, swapped


def after(value, *others):
    return lax.optimization_barrier((value, *others))[0]


def pool_matrix():
    lane = np.arange(2 * LANES)
    column = np.where(lane < LANES, lane // 2, LANES // 2 + (lane - LANES) // 2)
    return (np.arange(LANES)[None] == column[:, None]) * np.float32(0.125)


def spread_matrix(tall, broad):
    lane = np.arange(4 * tall * broad)
    tile, half, w = lane // LANES, lane % LANES // (2 * broad), lane % (2 * broad)
    row = tile + half * TILES
    cell = row // 2 * broad + w // 2
    return (np.arange(tall * broad)[:, None] == cell[None]) * np.float32(0.125)


def body(volume, w_three, w_four, cotangent):
    own_in, planes, cells = volume.shape
    mid = w_three.shape[1]
    c_mid = w_four.shape[0] // 27
    outs = w_four.shape[1]
    half_planes = planes // 2
    coarse = cells // 4
    filt = lax.axis_index("filt")
    which = filt.astype(jnp.int32).reshape(1)

    own = volume.transpose(1, 0, 2)
    edge = swap(jnp.stack([own[0], own[planes - 1]]))
    middle = swap(own[1 : planes - 1])
    low, high = to_next(own[planes - 1]), to_previous(own[0])
    plow, phigh = to_next(edge[1]), to_previous(edge[0])
    volumes = (own, low, high, plow, phigh, edge, middle)

    fine_forward, fine_backward, wide_forward = call(
        weights_kernel,
        [
            ((3, 3 * mid, 6 * own_in), BF),
            ((3, 6 * own_in, 3 * mid), BF),
            ((9, outs, 3 * c_mid), BF),
        ],
        "weights",
        inputs=2,
    )(w_three, w_four)
    pool = jnp.asarray(pool_matrix(), BF)
    unpool = jnp.asarray(pool_matrix().T, BF)
    spread = jnp.asarray(spread_matrix(HH // 4, WW // 4), BF)

    pooled, slope = call(
        forward_fine_kernel,
        [((half_planes, mid, coarse), BF), ((planes, mid, cells), BF)],
        "forward_fine",
        [pltpu.VMEM((planes + 2, 6 * own_in, (HH + 2) * LANES), BF)],
        scalars=1,
        inputs=9,
    )(which, *volumes, fine_forward, pool)

    pooled_peer = swap(pooled)
    pool_low = to_next(jnp.stack([pooled[half_planes - 1], pooled_peer[half_planes - 1]]))
    pool_high = to_previous(jnp.stack([pooled[0], pooled_peer[0]]))
    coarse_lanes = (TILES + 2) * LANES
    grad_four, coarse_windows, four_first, four_last = call(
        forward_coarse_kernel,
        [
            ((half_planes, outs, coarse), BF),
            ((half_planes + 2, 3 * c_mid, coarse_lanes), BF),
            ((outs, coarse), BF),
            ((outs, coarse), BF),
        ],
        "forward_coarse",
        scalars=1,
        inputs=7,
    )(
        which,
        pooled,
        pooled_peer,
        pool_low,
        pool_high,
        wide_forward,
        cotangent.reshape(outs, -1),
        spread,
    )

    four_low, four_high = to_next(four_last), to_previous(four_first)
    (coarse_kernel,) = call(
        kernel_grad_coarse_kernel,
        [((27 * c_mid, outs), BF)],
        "kernel_grad_coarse",
        [pltpu.VMEM((27 * c_mid, outs), F32)],
        inputs=2,
    )(coarse_windows, grad_four.reshape(half_planes * outs, coarse))
    coarse_sum = Sum(coarse_kernel)
    (own_back, peer_back), _ = beside(
        [coarse_sum],
        call(
            backward_coarse_kernel,
            [((half_planes, mid, coarse), F32), ((half_planes, mid, coarse), BF)],
            "backward_coarse",
            [pltpu.VMEM((half_planes + 2, 3 * outs, coarse_lanes), BF)],
            scalars=1,
            inputs=4,
        ),
        (which, grad_four, four_low, four_high, w_four),
    )
    _, (peer_back,) = beside([coarse_sum], lambda: (), (), [peer_back])

    grad_three, three_first, three_last = call(
        grad_fine_kernel,
        [((planes, mid, cells), BF), ((mid, cells), BF), ((mid, cells), BF)],
        "grad_fine",
        inputs=4,
    )(own_back, peer_back, slope, unpool)
    three_low, three_high = to_next(three_last), to_previous(three_first)
    fine_kernel = []
    cut = planes // 2 + 1
    for start, end in ((0, cut), (cut, planes + 2)):
        fine_kernel, _ = beside(
            [coarse_sum],
            call(
                functools.partial(kernel_grad_fine_kernel, start, end),
                [((54 * own_in, mid), F32)],
                f"kernel_grad_fine_{start}",
                [pltpu.VMEM((end - start, 6 * own_in, (HH + 2) * LANES), BF)],
                scalars=1,
                inputs=8 + len(fine_kernel),
            ),
            (which, *volumes, grad_three.reshape(planes * mid, cells), *fine_kernel),
        )
    fine_kernel = fine_kernel[0].astype(BF)

    fine_sum = Sum(fine_kernel.reshape(27 * own_in, 2 * mid))
    parts = 4
    rows = HH // parts
    owns, peers, theirs = [], [], []
    for part in range(parts):
        (mine, *theirs), came = beside(
            [fine_sum, coarse_sum],
            call(
                functools.partial(backward_fine_kernel, part * rows, rows),
                [((planes, own_in, rows * WW), F32), ((planes, own_in, rows * WW), BF)],
                f"backward_fine_{part}",
                [pltpu.VMEM((planes + 2, 3 * mid, (rows + 2) * LANES), BF)],
                scalars=1,
                inputs=4,
            ),
            (which, grad_three, three_low, three_high, fine_backward),
            theirs,
        )
        owns.append(mine)
        peers += came
    _, came = beside([fine_sum, coarse_sum], lambda: (), (), theirs)
    peers += came
    coarse_sum = coarse_sum.finish()
    fine_sum = fine_sum.finish().reshape(54 * own_in, mid)
    x_grad = jnp.concatenate([a + b.astype(F32) for a, b in zip(owns, peers)], axis=2)
    x_grad = x_grad.transpose(1, 0, 2)

    all_cells = planes * lax.axis_size("depth") * cells
    scale_four = 1.0 / math.sqrt(all_cells / 8.0)
    scale_three = 1.0 / math.sqrt(all_cells * 1.0)
    return (x_grad, fine_sum.astype(F32) * scale_three, coarse_sum.astype(F32) * scale_four)


def solution(mesh):
    return jax.shard_map(
        body,
        mesh=mesh,
        in_specs=(
            P("filt", "depth", None),
            P(None, "filt"),
            P(None, "filt"),
            P("filt", "depth", None),
        ),
        out_specs=(P("filt", "depth", None), P(None, "filt"), P(None, "filt")),
        check_vma=False,
    )
```

```python
import functools
import math

import jax
import jax.numpy as jnp
import numpy as np
from jax import lax
from jax.experimental import pallas as pl
from jax.experimental.pallas import tpu as pltpu
from jax.sharding import PartitionSpec as P

HH = 32
WW = 128
LANES = 128
BF = jnp.bfloat16
F32 = jnp.float32
TILES = HH // 4
ROWS = 16


def nn(a, b):
    return jnp.dot(a, b, preferred_element_type=F32)


def nt(a, b):
    return lax.dot_general(a, b, (((1,), (1,)), ((), ())), preferred_element_type=F32)


def call(body, outs, name, scratch=(), scalars=0, inputs=0, mib=12):
    specs = [pl.BlockSpec(memory_space=pltpu.SMEM)] * scalars
    specs += [pl.BlockSpec(memory_space=pltpu.VMEM)] * inputs
    return pl.pallas_call(
        body,
        out_shape=[jax.ShapeDtypeStruct(shape, dtype) for shape, dtype in outs],
        in_specs=specs,
        out_specs=[pl.BlockSpec(memory_space=pltpu.VMEM)] * len(outs),
        scratch_shapes=list(scratch),
        compiler_params=pltpu.CompilerParams(vmem_limit_bytes=mib * 2**20),
        name=name,
    )


def sigmoid(value):
    return 0.5 * jnp.tanh(0.5 * value) + 0.5


def shifted(block, width):
    lane = lax.broadcasted_iota(jnp.int32, block.shape, 1) % width
    zero = jnp.zeros(block.shape, BF)
    before = jnp.where(lane == 0, zero, pltpu.roll(block, 1, axis=1))
    after = jnp.where(lane == width - 1, zero, pltpu.roll(block, LANES - 1, axis=1))
    return before, after


def fine_rows(source, windows, plane, offset, chans, group, first, lower, upper):

    def row(step):
        block = source(step)
        before, after = shifted(block, WW)
        lanes = pl.ds(pl.multiple_of((step - first + 1) * LANES, LANES), LANES)
        for shift, value in enumerate((before, block, after)):
            windows[plane, pl.ds(pl.multiple_of(shift * group + offset, 32), chans), lanes] = value

    def several(turn, _):
        for k in range(ROWS):
            row(lower + turn * ROWS + k)
        return 0

    zero = jnp.zeros((chans, LANES), BF)
    for shift in range(3):
        rows = pl.ds(pl.multiple_of(shift * group + offset, 32), chans)
        if lower == 0 and first == 0:
            windows[plane, rows, 0:LANES] = zero
        if upper == HH:
            windows[plane, rows, (HH + 1 - first) * LANES : (HH + 2 - first) * LANES] = zero
    if upper - lower >= ROWS:
        lax.fori_loop(0, (upper - lower) // ROWS, several, 0)
    for step in range(upper - (upper - lower) % ROWS, upper):
        row(step)


def row_of(ref, base=0):
    def source(step):
        return ref[:, pl.ds(pl.multiple_of((step - base) * LANES, LANES), LANES)]

    return source


def coarse_rows(source, windows, plane, offset, chans, group):
    half = LANES // 2
    lane = lax.broadcasted_iota(jnp.int32, (chans, LANES), 1)

    def put(shift, tile, value):
        rows = pl.ds(pl.multiple_of(shift * group + offset, 32), chans)
        windows[plane, rows, tile * LANES : (tile + 1) * LANES] = value

    for tile in range(TILES):
        block = source(tile)
        before, after = shifted(block, half)
        for shift, value in enumerate((before, block, after)):
            put(shift, tile + 1, value)
            if tile == 0 or tile == TILES - 1:
                turned = pltpu.roll(value.astype(F32), half, axis=1)
                if tile == TILES - 1:
                    put(shift, 0, jnp.where(lane < half, 0.0, turned).astype(BF))
                else:
                    put(shift, TILES + 1, jnp.where(lane < half, turned, 0.0).astype(BF))


def tile_of(ref):
    def source(tile):
        return ref[:, tile * LANES : (tile + 1) * LANES]

    return source


def each(count, build):
    def step(d, _):
        build(d)
        return 0

    lax.fori_loop(0, count, step, 0)


def volume_windows(filt, refs, windows, first, last):
    own, low, high, peer_low, peer_high, edge, middle = refs
    planes, chans, _ = own.shape
    mine = pl.multiple_of(filt[0] * chans, 32)
    theirs = pl.multiple_of((1 - filt[0]) * chans, 32)

    def put(ref, plane, offset):
        fine_rows(row_of(ref), windows, plane - first, offset, chans, 2 * chans, 0, 0, HH)

    lower, upper = max(first, 1), min(last, planes + 1)
    each(upper - lower, lambda d: put(own.at[d + lower - 1], d + lower, mine))
    lower, upper = max(first, 2), min(last, planes)
    each(upper - lower, lambda d: put(middle.at[d + lower - 2], d + lower, theirs))
    if first == 0 and last == planes + 2:
        each(2, lambda d: put(edge.at[d], 1 + d * (planes - 1), theirs))
    elif first == 0:
        put(edge.at[0], 1, theirs)
    else:
        put(edge.at[1], planes, theirs)
    if first == 0:
        put(low, 0, mine)
        put(peer_low, 0, theirs)
    if last == planes + 2:
        put(high, planes + 1, mine)
        put(peer_high, planes + 1, theirs)


def forward_fine_kernel(filt, *refs):
    weights, pool, pooled, slope, windows = refs[-5:]
    planes = refs[0].shape[0]
    volume_windows(filt, refs[:-5], windows, 0, planes + 2)
    outs = weights.shape[1] // 3
    span = 2 * LANES

    def chunk(j, _):
        acts = [[None, None] for _ in range(planes)]
        for side in range(2):
            top = side * (HH // 2) + j * 2
            totals = [None] * planes
            for p in range(planes + 2):
                value = None
                for kh in range(3):
                    lanes = pl.ds(pl.multiple_of((top + kh) * LANES, LANES), span)
                    part = nn(weights[kh], windows[p, :, lanes])
                    value = part if value is None else value + part
                for kd in range(3):
                    d = p - kd
                    if 0 <= d < planes:
                        piece = value[kd * outs : (kd + 1) * outs]
                        totals[d] = piece if totals[d] is None else totals[d] + piece
            for d in range(planes):
                pre = totals[d]
                sigma = sigmoid(pre)
                act = pre * sigma
                slope[d, :, pl.ds(pl.multiple_of(top * LANES, LANES), span)] = (
                    sigma + act * (1.0 - sigma)
                ).astype(BF)
                acts[d][side] = act[:, :LANES] + act[:, LANES:]
        for d in range(0, planes, 2):
            both = jnp.concatenate(
                [acts[d][0] + acts[d + 1][0], acts[d][1] + acts[d + 1][1]], axis=1
            )
            coarse = both.astype(BF)
            rest = (both - coarse.astype(F32)).astype(BF)
            mean = nn(coarse, pool[...]) + nn(rest, pool[...])
            pooled[d // 2, :, pl.ds(pl.multiple_of(j * LANES, LANES), LANES)] = mean.astype(BF)
        return 0

    lax.fori_loop(0, TILES, chunk, 0, unroll=2)


def forward_coarse_kernel(filt, own, peer, low, high, plow, phigh, weights, cot, spread, grads, windows, first_out, last_out):
    planes, chans, cells = own.shape
    mine = pl.multiple_of(filt[0] * chans, 32)
    theirs = pl.multiple_of((1 - filt[0]) * chans, 32)
    sides = ((mine, low, own, high), (theirs, plow, peer, phigh))
    for offset, below, middle, above in sides:
        refs = [below] + [middle.at[d] for d in range(planes)] + [above]
        for plane, ref in enumerate(refs):
            coarse_rows(tile_of(ref), windows, plane, offset, chans, 2 * chans)
    upper = nn(cot[...], spread[...])
    span = cells // 2
    for d in range(planes):
        for start in range(0, cells, span):
            pre = None
            for kd in range(3):
                for kh in range(3):
                    begin = start + kh * LANES
                    part = nn(weights[kd * 3 + kh], windows[d + kd, :, begin : begin + span])
                    pre = part if pre is None else pre + part
            sigma = sigmoid(pre)
            slope = sigma * (1.0 + pre * (1.0 - sigma))
            value = (upper[:, start : start + span] * slope).astype(BF)
            grads[d, :, start : start + span] = value
            if d == 0:
                first_out[:, start : start + span] = value
            if d == planes - 1:
                last_out[:, start : start + span] = value


def kernel_grad_coarse_kernel(windows, grads, out, total):
    deep, group, _ = windows.shape
    planes = deep - 2
    outs = grads.shape[0] // planes
    cells = grads.shape[1]
    seen = set()
    for p in range(deep):
        first, last = max(p - 2, 0), min(p, planes - 1)
        for kh in range(3):
            value = nt(
                windows[p, :, kh * LANES : kh * LANES + cells],
                grads[first * outs : (last + 1) * outs, :],
            )
            for d in range(first, last + 1):
                index = (p - d) * 3 + kh
                rows = slice(index * group, (index + 1) * group)
                part = value[:, (d - first) * outs : (d - first + 1) * outs]
                total[rows, :] = total[rows, :] + part if index in seen else part
                seen.add(index)
    out[...] = total[...].astype(out.dtype)


def pick(filt, value):
    half = value.shape[0] // 2
    first = filt[0] == 0
    return (
        jnp.where(first, value[:half], value[half:]),
        jnp.where(first, value[half:], value[:half]),
    )


def backward_coarse_kernel(filt, grads, low, high, weights, own, peer, windows):
    planes, chans, cells = grads.shape
    refs = [low] + [grads.at[d] for d in range(planes)] + [high]
    for plane, ref in enumerate(refs):
        coarse_rows(tile_of(ref), windows, plane, 0, chans, chans)
    rows = weights.shape[0] // 27
    span = cells // 2
    for d in range(planes):
        for start in range(0, cells, span):
            value = None
            for kd in range(3):
                for kh in range(3):
                    base = ((2 - kd) * 9 + (2 - kh) * 3) * rows
                    taps = jnp.concatenate(
                        [weights[base + k * rows : base + (k + 1) * rows, :] for k in (2, 1, 0)],
                        axis=1,
                    )
                    begin = start + kh * LANES
                    part = nn(taps, windows[d + kd, :, begin : begin + span])
                    value = part if value is None else value + part
            mine, theirs = pick(filt, value)
            own[d, :, start : start + span] = mine
            peer[d, :, start : start + span] = theirs.astype(BF)


def weights_kernel(fine, wide, fine_forward, fine_backward, wide_forward):
    chans = fine.shape[0] // 27
    outs = fine.shape[1]
    for kd in range(3):
        for kh in range(3):
            base = (kd * 3 + kh) * 3 * chans
            block = fine[base : base + 3 * chans, :].astype(F32).T
            fine_forward[kh, kd * outs : (kd + 1) * outs, :] = block.astype(BF)
            base = ((2 - kd) * 9 + (2 - kh) * 3) * chans
            fine_backward[kh, kd * chans : (kd + 1) * chans, :] = jnp.concatenate(
                [fine[base + k * chans : base + (k + 1) * chans, :] for k in (2, 1, 0)], axis=1
            )
    group = wide.shape[0] // 9
    for k in range(9):
        block = wide[k * group : (k + 1) * group, :].astype(F32).T
        wide_forward[k] = block.astype(BF)


def grad_fine_kernel(own, peer, slope, unpool, grads, first_out, last_out):
    planes = own.shape[0]
    for d in range(planes):
        for j in range(TILES):
            lanes = slice(j * LANES, (j + 1) * LANES)
            block = (own[d, :, lanes] + peer[d, :, lanes].astype(F32)).astype(BF)
            wide = nn(block, unpool[...])
            for side in range(2):
                part = wide[:, side * LANES : (side + 1) * LANES]
                for a in range(2):
                    for row in (side * HH // 2 + 2 * j, side * HH // 2 + 2 * j + 1):
                        cells = slice(row * LANES, (row + 1) * LANES)
                        factor = slope[2 * d + a, :, cells].astype(F32)
                        value = (part * factor).astype(BF)
                        grads[2 * d + a, :, cells] = value
                        if 2 * d + a == 0:
                            first_out[:, cells] = value
                        if 2 * d + a == 2 * planes - 1:
                            last_out[:, cells] = value


def kernel_grad_fine_kernel(start, end, filt, *refs):
    grads = refs[7]
    out, windows = refs[-2:]
    before = refs[8] if start > 0 else None
    planes, _, cells = refs[0].shape
    volume_windows(filt, refs[:7], windows, start, end)
    group = windows.shape[1]
    outs = grads.shape[0] // planes
    seen = set()
    for p in range(start, end):
        first, last = max(p - 2, 0), min(p, planes - 1)
        for kh in range(3):
            value = nt(
                windows[p - start, :, kh * LANES : kh * LANES + cells],
                grads[first * outs : (last + 1) * outs, :],
            )
            for d in range(first, last + 1):
                index = (p - d) * 3 + kh
                rows = slice(index * group, (index + 1) * group)
                part = value[:, (d - first) * outs : (d - first + 1) * outs]
                if index in seen:
                    part = out[rows, :] + part
                elif before is not None:
                    part = before[rows, :] + part
                out[rows, :] = part
                seen.add(index)


def backward_fine_kernel(first, count, filt, grads, low, high, weights, own, peer, windows):
    planes, chans, _ = grads.shape

    def put(ref, plane):
        lower, upper = max(first - 1, 0), min(first + count + 1, HH)
        fine_rows(row_of(ref), windows, plane, 0, chans, chans, first, lower, upper)

    each(planes, lambda d: put(grads.at[d], d + 1))
    put(low, 0)
    put(high, planes + 1)
    outs = weights.shape[1] // 3
    span = 2 * LANES

    def chunk(j, _):
        totals = [None] * planes
        for p in range(planes + 2):
            value = None
            for kh in range(3):
                lanes = pl.ds(pl.multiple_of((2 * j + kh) * LANES, LANES), span)
                part = nn(weights[kh], windows[p, :, lanes])
                value = part if value is None else value + part
            for kd in range(3):
                d = p - kd
                if 0 <= d < planes:
                    piece = value[kd * outs : (kd + 1) * outs]
                    totals[d] = piece if totals[d] is None else totals[d] + piece
        cells = pl.ds(pl.multiple_of(j * span, span), span)
        for d in range(planes):
            mine, theirs = pick(filt, totals[d])
            own[d, :, cells] = mine
            peer[d, :, cells] = theirs.astype(BF)
        return 0

    lax.fori_loop(0, count // 2, chunk, 0, unroll=2)


def to_next(value):
    count = lax.axis_size("depth")
    return lax.ppermute(value, "depth", [(i, i + 1) for i in range(count - 1)])


def to_previous(value):
    count = lax.axis_size("depth")
    return lax.ppermute(value, "depth", [(i + 1, i) for i in range(count - 1)])


def swap(value):
    return lax.ppermute(value, "filt", [(0, 1), (1, 0)])


def halves(value, bit):
    upper = (lax.axis_index("depth") & bit) != 0
    half = value.shape[0] // 2
    return (
        jnp.where(upper, value[half:], value[:half]),
        jnp.where(upper, value[:half], value[half:]),
    )


def across(value, bit):
    count = lax.axis_size("depth")
    return lax.ppermute(value, "depth", [(i, i ^ bit) for i in range(count)])


def plus(a, b):
    return (a.astype(F32) + b.astype(F32)).astype(a.dtype)


def depth_sum(value):
    count = lax.axis_size("depth")
    rows = value.shape[0]
    value = jnp.pad(value, ((0, -rows % 64), (0, 0)))
    near = [bit for bit in (1, 2) if bit < count]
    for bit in near:
        keep, send = halves(value, bit)
        other = yield send, bit
        value = plus(keep, other)
    bit = 4
    while bit < count:
        other = yield value, bit
        value = plus(value, other)
        bit *= 2
    for bit in reversed(near):
        other = yield value, bit
        upper = (lax.axis_index("depth") & bit) != 0
        value = jnp.concatenate(
            [jnp.where(upper, other, value), jnp.where(upper, value, other)], axis=0
        )
    return value[:rows]


class Sum:
    def __init__(self, value):
        self.steps = depth_sum(value)
        self.result = None
        self.take(None)

    def take(self, other):
        try:
            self.pending = self.steps.send(other)
        except StopIteration as stop:
            self.pending, self.result = None, stop.value

    def finish(self):
        while self.pending is not None:
            self.take(across(*self.pending))
        return self.result


def beside(sums, kernel, inputs, swapped=()):
    sums = [one for one in sums if one.pending is not None]
    sends = [one.pending[0] for one in sums]
    inputs, sends, swapped = lax.optimization_barrier((list(inputs), sends, list(swapped)))
    others = [across(send, one.pending[1]) for send, one in zip(sends, sums)]
    swapped = [swap(value) for value in swapped]
    outs, others, swapped = lax.optimization_barrier((kernel(*inputs), others, swapped))
    for one, other in zip(sums, others):
        one.take(other)
    return outs, swapped


def after(value, *others):
    return lax.optimization_barrier((value, *others))[0]


def pool_matrix():
    lane = np.arange(2 * LANES)
    column = np.where(lane < LANES, lane // 2, LANES // 2 + (lane - LANES) // 2)
    return (np.arange(LANES)[None] == column[:, None]) * np.float32(0.125)


def spread_matrix(tall, broad):
    lane = np.arange(4 * tall * broad)
    tile, half, w = lane // LANES, lane % LANES // (2 * broad), lane % (2 * broad)
    row = tile + half * TILES
    cell = row // 2 * broad + w // 2
    return (np.arange(tall * broad)[:, None] == cell[None]) * np.float32(0.125)


def body(volume, w_three, w_four, cotangent):
    own_in, planes, cells = volume.shape
    mid = w_three.shape[1]
    c_mid = w_four.shape[0] // 27
    outs = w_four.shape[1]
    half_planes = planes // 2
    coarse = cells // 4
    filt = lax.axis_index("filt")
    which = filt.astype(jnp.int32).reshape(1)

    own = volume.transpose(1, 0, 2)
    edge = swap(jnp.stack([own[0], own[planes - 1]]))
    middle = swap(own[1 : planes - 1])
    low, high = to_next(own[planes - 1]), to_previous(own[0])
    plow, phigh = to_next(edge[1]), to_previous(edge[0])
    volumes = (own, low, high, plow, phigh, edge, middle)

    fine_forward, fine_backward, wide_forward = call(
        weights_kernel,
        [
            ((3, 3 * mid, 6 * own_in), BF),
            ((3, 6 * own_in, 3 * mid), BF),
            ((9, outs, 3 * c_mid), BF),
        ],
        "weights",
        inputs=2,
    )(w_three, w_four)
    pool = jnp.asarray(pool_matrix(), BF)
    unpool = jnp.asarray(pool_matrix().T, BF)
    spread = jnp.asarray(spread_matrix(HH // 4, WW // 4), BF)

    pooled, slope = call(
        forward_fine_kernel,
        [((half_planes, mid, coarse), BF), ((planes, mid, cells), BF)],
        "forward_fine",
        [pltpu.VMEM((planes + 2, 6 * own_in, (HH + 2) * LANES), BF)],
        scalars=1,
        inputs=9,
        mib=20,
    )(which, *volumes, fine_forward, pool)

    pooled_peer = swap(pooled)
    pool_low, pool_high = to_next(pooled[half_planes - 1]), to_previous(pooled[0])
    peer_low, peer_high = to_next(pooled_peer[half_planes - 1]), to_previous(pooled_peer[0])
    coarse_lanes = (TILES + 2) * LANES
    grad_four, coarse_windows, four_first, four_last = call(
        forward_coarse_kernel,
        [
            ((half_planes, outs, coarse), BF),
            ((half_planes + 2, 3 * c_mid, coarse_lanes), BF),
            ((outs, coarse), BF),
            ((outs, coarse), BF),
        ],
        "forward_coarse",
        scalars=1,
        inputs=9,
    )(
        which,
        pooled,
        pooled_peer,
        pool_low,
        pool_high,
        peer_low,
        peer_high,
        wide_forward,
        cotangent.reshape(outs, -1),
        spread,
    )

    four_low, four_high = to_next(four_last), to_previous(four_first)
    (coarse_kernel,) = call(
        kernel_grad_coarse_kernel,
        [((27 * c_mid, outs), BF)],
        "kernel_grad_coarse",
        [pltpu.VMEM((27 * c_mid, outs), F32)],
        inputs=2,
    )(coarse_windows, grad_four.reshape(half_planes * outs, coarse))
    coarse_sum = Sum(coarse_kernel)
    (own_back, peer_back), _ = beside(
        [coarse_sum],
        call(
            backward_coarse_kernel,
            [((half_planes, mid, coarse), F32), ((half_planes, mid, coarse), BF)],
            "backward_coarse",
            [pltpu.VMEM((half_planes + 2, 3 * outs, coarse_lanes), BF)],
            scalars=1,
            inputs=4,
        ),
        (which, grad_four, four_low, four_high, w_four),
    )
    _, (peer_back,) = beside([coarse_sum], lambda: (), (), [peer_back])

    grad_three, three_first, three_last = call(
        grad_fine_kernel,
        [((planes, mid, cells), BF), ((mid, cells), BF), ((mid, cells), BF)],
        "grad_fine",
        inputs=4,
    )(own_back, peer_back, slope, unpool)
    three_low, three_high = to_next(three_last), to_previous(three_first)
    fine_kernel = []
    cut = planes // 2 + 1
    for start, end in ((0, cut), (cut, planes + 2)):
        fine_kernel, _ = beside(
            [coarse_sum],
            call(
                functools.partial(kernel_grad_fine_kernel, start, end),
                [((54 * own_in, mid), F32)],
                f"kernel_grad_fine_{start}",
                [pltpu.VMEM((end - start, 6 * own_in, (HH + 2) * LANES), BF)],
                scalars=1,
                inputs=8 + len(fine_kernel),
                mib=16,
            ),
            (which, *volumes, grad_three.reshape(planes * mid, cells), *fine_kernel),
        )
    fine_kernel = fine_kernel[0].astype(BF)

    fine_sum = Sum(fine_kernel.reshape(27 * own_in, 2 * mid))
    parts = 4
    rows = HH // parts
    owns, peers, theirs = [], [], []
    for part in range(parts):
        (mine, *theirs), came = beside(
            [fine_sum, coarse_sum],
            call(
                functools.partial(backward_fine_kernel, part * rows, rows),
                [((planes, own_in, rows * WW), F32), ((planes, own_in, rows * WW), BF)],
                f"backward_fine_{part}",
                [pltpu.VMEM((planes + 2, 3 * mid, (rows + 2) * LANES), BF)],
                scalars=1,
                inputs=4,
            ),
            (which, grad_three, three_low, three_high, fine_backward),
            theirs,
        )
        owns.append(mine)
        peers += came
    _, came = beside([fine_sum, coarse_sum], lambda: (), (), theirs)
    peers += came
    coarse_sum = coarse_sum.finish()
    fine_sum = fine_sum.finish().reshape(54 * own_in, mid)
    x_grad = jnp.concatenate([a + b.astype(F32) for a, b in zip(owns, peers)], axis=2)
    x_grad = x_grad.transpose(1, 0, 2)

    all_cells = planes * lax.axis_size("depth") * cells
    scale_four = 1.0 / math.sqrt(all_cells / 8.0)
    scale_three = 1.0 / math.sqrt(all_cells * 1.0)
    return (x_grad, fine_sum.astype(F32) * scale_three, coarse_sum.astype(F32) * scale_four)


def solution(mesh):
    return jax.shard_map(
        body,
        mesh=mesh,
        in_specs=(
            P("filt", "depth", None),
            P(None, "filt"),
            P(None, "filt"),
            P("filt", "depth", None),
        ),
        out_specs=(P("filt", "depth", None), P(None, "filt"), P(None, "filt")),
        check_vma=False,
    )
```
